256 devices in a mesh: ctx: 32 (over x, z), tp: 8 (over y, core).
Axes of the slice: x: 4, y: 4, z: 8, core: 2. Of those that a mesh axis runs over, the one named last changes fastest.
Arguments:
- hidden_in: bfloat16 [16384, 4096], P('ctx', 'tp'), may hold values from -6 to 6
- w_qkv: bfloat16 [3, 4096, 2048], P(None, None, 'tp'), may hold values from -0.09375 to 0.09375
- lr_weight: bfloat16 [4096, 16], P(None, 'tp'), may hold values from -0.09375 to 0.09375
- inner_lr: float32 [16], P('tp'), may hold values from 0.0005 to 0.5
- init_state: float32 [16, 128, 128], P('tp'), may hold values from -0.5 to 0.5
- norm_gain: float32 [16, 128], P('tp'), may hold values from 0.1 to 1.9
- w_out: bfloat16 [2048, 4096], P('tp'), may hold values from -0.125 to 0.125
Outputs:
- mixed: bfloat16 [16384, 4096], P('ctx', 'tp')
The draws below stay inside these ranges and needn't reach their ends.
All inputs are finite; a program needn't handle non-finite values.
Results may differ from the reference program's by a relative error of at most 0.019.
Values may be sent and summed in bfloat16 or wider, within the bound.
A program may use at most 64 MiB of HBM per device.

```python
import math
import jax
import jax.numpy as jnp
from jax import lax

D = 4096
HEADS = 16
HD = 128
MB = 16
TOKENS = 16384


def block_levels(stream_key, dims, cuts, smallest, high):
    level, own = 1.0, jax.random.fold_in(stream_key, 6)
    for dim, parts in cuts:
        heights = jnp.exp(jax.random.uniform(jax.random.fold_in(own, dim), (parts,), jnp.float32, smallest / len(cuts), high / len(cuts)))
        level = level * jnp.repeat(heights, dims[dim] // parts).reshape([-1 if axis == dim else 1 for axis in range(len(dims))])
    return level


def noise(rng, extent, deviation, most, split=(), held_as=jnp.bfloat16):
    array = jax.random.normal(rng, extent, jnp.float32) * deviation
    if len(split) > 0:
        array = block_levels(rng, extent, split, -0.22, 0.18) * array
    return jnp.clip(array, min=-most, max=most).astype(held_as)


def setup_inputs(seed: int = 0) -> dict:
    streams_of = jax.random.split(jax.random.key(seed), 8)
    return {
        "hidden_in": noise(streams_of[0], (TOKENS, D), 1.0, 6.0, ((0, 32), (1, 8))),
        "w_qkv": noise(streams_of[1], (3, D, HEADS * HD), D ** -0.5, 0.09375, ((2, 8),)),
        "lr_weight": noise(streams_of[2], (D, HEADS), D ** -0.5, 0.09375, ((1, 8),)),
        "inner_lr": jnp.clip(jnp.exp(math.log(0.5) - 6.9077552 * jax.random.uniform(streams_of[3], (HEADS,), jnp.float32) ** block_levels(streams_of[3], (HEADS,), ((0, 8),), -0.2, 0.2)), 0.0005, 0.5),
        "init_state": noise(streams_of[4], (HEADS, HD, HD), HD ** -0.5, 0.5, ((0, 8),), jnp.float32),
        "norm_gain": jnp.clip(1.0 + 0.18 * jax.random.normal(streams_of[5], (HEADS, HD), jnp.float32), 0.1, 1.9),
        "w_out": noise(streams_of[6], (HEADS * HD, D), (HEADS * HD) ** -0.5, 0.125, ((0, 8),)),
    }


def normalize(v):
    return v / jnp.sqrt(v.shape[-1] * (lax.optimization_barrier(jnp.mean(v * v, -1, keepdims=True)) + 1e-06))

def mm(form, a, b):
    return jnp.einsum(form, a, b, precision=lax.Precision.HIGHEST)

def reference(hidden_in, w_qkv, lr_weight, inner_lr, init_state, norm_gain, w_out):
    proj = jnp.einsum('td,cdj->ctj', hidden_in.astype(jnp.float32), w_qkv.astype(jnp.float32), precision=lax.Precision.HIGHEST)
    logit = jnp.dot(hidden_in, lr_weight, preferred_element_type=jnp.float32)
    rate = inner_lr[:, None] * jax.nn.sigmoid(logit).T

    def split_heads(m):
        return m.reshape(TOKENS, HEADS, HD).transpose(1, 0, 2)
    queries = normalize(split_heads(proj[0]))
    keys = normalize(split_heads(proj[1]))
    values = split_heads(proj[2])
    nblk = TOKENS // MB

    def blocks(m):
        return m.reshape(HEADS, nblk, MB, HD).transpose(1, 0, 2, 3)
    rate_blocks = rate.reshape(HEADS, nblk, MB).transpose(1, 0, 2)
    lower = jnp.tril(jnp.ones((MB, MB), jnp.float32))

    def step(state, block):
        qb, kb, vb, rb = block
        err = mm('hsi,hij->hsj', kb, state) - vb
        scores = mm('hti,hsi->hts', qb, kb) * lower * rb[:, None, :]
        outz = mm('hti,hij->htj', qb, state) - mm('hts,hsj->htj', scores, err)
        state = state - mm('hsi,hsj->hij', kb, rb[:, :, None] * err)
        return (state, outz)
    final, zvals = lax.scan(step, init_state, (blocks(queries), blocks(keys), blocks(values), rate_blocks))
    zvals = zvals.transpose(0, 2, 1, 3).reshape(TOKENS, HEADS, HD)
    normed = zvals / jnp.sqrt(lax.optimization_barrier(jnp.mean(zvals * zvals, -1, keepdims=True)) + 1e-06) * norm_gain
    normed = normed.reshape(TOKENS, HEADS * HD).astype(jnp.bfloat16)
    return jnp.dot(normed, w_out, preferred_element_type=jnp.float32).astype(jnp.bfloat16)
```

```python
import jax
import jax.numpy as jnp
from jax import lax
from jax.experimental import pallas as pl
from jax.experimental.pallas import tpu as pltpu
from jax.sharding import PartitionSpec as P

MB = 16
CH = 128
MESH = pl.DeviceIdType.MESH
F32 = jnp.float32
BF16 = jnp.bfloat16
Y, CORES = 4, 2
X, Z = 4, 8


def dot(a, b):
    return jnp.dot(a.astype(BF16), b.astype(BF16), preferred_element_type=F32)


def compose(later, earlier, hd):
    return earlier + dot(later[:, :hd], earlier) + later


def apply_map(m, w, hd):
    return w + dot(m[:, :hd], w) + m[:, hd:]


def gather_kernel(hid, wq, lrw, lr, p_out, n_out, x_out, xg, wbuf, lrt, pref, loc, send, recv, wsem):
    rows, feat = hid.shape
    nc = rows // CH
    half = CH // 2
    hd = x_out.shape[1]
    heads = x_out.shape[0]
    width = heads * hd
    me = lax.axis_index("tp")
    ring = Y * CORES
    sib = me + 1 - 2 * lax.rem(me, 2)
    up = lax.rem(me + 2, ring)
    down = lax.rem(me + ring - 2, ring)
    opp = lax.rem(me + 4, ring)

    barrier = pltpu.get_barrier_semaphore()
    for peer in (sib, up, down):
        pl.semaphore_signal(barrier, inc=1, device_id={"tp": peer}, device_id_type=MESH)

    wcopies = [
        pltpu.make_async_copy(wq.at[c], wbuf.at[:, pl.ds(c * width, width)], wsem.at[c]) for c in range(3)
    ]
    for cp in wcopies:
        cp.start()

    def cols(j):
        return pl.ds(pl.multiple_of(j * feat, feat), feat)

    def transfer(kind, c):
        if kind < 3:
            src, r0, n, owner = hid, 0, CH, me
        elif kind in (3, 5):
            src, r0, n, owner = xg, 0, (half if kind == 3 else CH), down
        elif kind in (4, 6):
            src, r0, n, owner = xg, (half if kind == 4 else 0), (half if kind == 4 else CH), up
        else:
            src, r0, n, owner = xg, (0 if kind == 7 else half), half, opp
        to = {0: up, 1: down, 3: up, 4: down}.get(kind, sib)
        rs = pl.ds(pl.multiple_of(c * CH + r0, 16), n)
        source = hid.at[rs] if kind < 3 else xg.at[rs, cols(owner)]
        return pltpu.make_async_remote_copy(
            src_ref=source,
            dst_ref=xg.at[rs, cols(owner)],
            send_sem=send.at[c, kind],
            recv_sem=recv.at[c, kind],
            device_id={"tp": to},
            device_id_type=MESH,
        )

    def arrival(kind, c):
        owner = {0: down, 1: up, 2: sib, 3: opp, 4: opp, 5: lax.rem(sib + ring - 2, ring),
                 6: lax.rem(sib + 2, ring), 7: lax.rem(sib + 4, ring), 8: lax.rem(sib + 4, ring)}[kind]
        r0 = half if kind in (4, 8) else 0
        n = half if kind in (3, 4, 7, 8) else CH
        rs = pl.ds(pl.multiple_of(c * CH + r0, 16), n)
        dst = xg.at[rs, cols(owner)]
        return pltpu.make_async_remote_copy(
            src_ref=dst, dst_ref=dst, send_sem=send.at[c, kind], recv_sem=recv.at[c, kind],
            device_id={"tp": sib}, device_id_type=MESH,
        )

    def begin(c):
        for kind in range(3):
            transfer(kind, c).start()

    def forward(c):
        arrival(0, c).wait_recv()
        transfer(3, c).start()
        transfer(5, c).start()
        arrival(1, c).wait_recv()
        transfer(4, c).start()
        transfer(6, c).start()

    def forward_opposite(c):
        arrival(3, c).wait_recv()
        transfer(7, c).start()
        arrival(4, c).wait_recv()
        transfer(8, c).start()

    pl.semaphore_wait(barrier, 3)
    begin(0)
    begin(1)
    own = pltpu.make_async_copy(hid, xg.at[:, cols(me)], loc)
    own.start()

    lrt[...] = jnp.zeros_like(lrt)
    lrt[0:heads, :] = lrw[...].astype(F32)
    for i in range(wbuf.shape[0] // CH):
        wbuf[i * CH:(i + 1) * CH, 3 * width:] = lrt[:, i * CH:(i + 1) * CH].T.astype(BF16)
    pref[...] = jnp.zeros_like(pref)
    own.wait()
    forward(0)
    forward_opposite(0)
    for cp in wcopies:
        cp.wait()

    row = lax.broadcasted_iota(jnp.int32, (CH, CH), 0)
    col = lax.broadcasted_iota(jnp.int32, (CH, CH), 1)
    causal = row >= col
    before = (row >> 4) > (col >> 4)

    def chunk(c, carry):
        @pl.when(c < nc - 2)
        def _():
            begin(c + 2)

        @pl.when(c < nc - 1)
        def _():
            forward(c + 1)

        for kind in (2, 5, 6, 7, 8):
            arrival(kind, c).wait_recv()
        rs = pl.ds(pl.multiple_of(c * CH, CH), CH)
        proj = jnp.dot(xg[rs, :], wbuf[...], preferred_element_type=F32)

        @pl.when(c < nc - 1)
        def _():
            forward_opposite(c + 1)

        hs = range(heads)
        part = [[proj[:, (k * heads + h) * hd:(k * heads + h + 1) * hd] for h in hs] for k in range(3)]

        def unit(v):
            return v * lax.rsqrt(jnp.sum(v * v, -1, keepdims=True) + hd * 1e-06)

        q = [unit(part[0][h]) for h in hs]
        k = [unit(part[1][h]) for h in hs]
        rate = [lr[h] * jax.nn.sigmoid(proj[:, 3 * width + h:3 * width + h + 1]) for h in hs]
        krt = [(k[h] * rate[h]).T.astype(BF16) for h in hs]
        sg = [dot(jnp.concatenate([q[h], k[h]], 0), krt[h]) for h in hs]
        m = [jnp.where(causal, sg[h][:CH], 0.0).astype(BF16) for h in hs]
        l1 = [jnp.where(before, sg[h][CH:], 0.0) for h in hs]
        lb = [l1[h].astype(BF16) for h in hs]
        l2 = [dot(lb[h], lb[h]) for h in hs]
        l34 = [dot(jnp.concatenate([lb[h], l2[h].astype(BF16)], 0), l2[h]) for h in hs]
        t1 = [l2[h] - l1[h] - l34[h][:CH] for h in hs]
        t = [t1[h] + l34[h][CH:] + dot(t1[h], l34[h][CH:]) for h in hs]
        kv = [jnp.concatenate([k[h], part[2][h]], 1) for h in hs]
        uy = [kv[h] + dot(t[h], kv[h]) for h in hs]
        dn = [dot(jnp.concatenate([krt[h], m[h]], 0), uy[h]) for h in hs]
        d = [jnp.concatenate([-dn[h][:CH, :hd], dn[h][:CH, hd:]], 1) for h in hs]
        p = [q[h] - dn[h][CH:, :hd] for h in hs]
        n = [dn[h][CH:, hd:] for h in hs]
        x0 = [pref[h] for h in hs]
        dx = [dot(jnp.concatenate([d[h][:, :hd], p[h]], 0), x0[h]) for h in hs]
        for h in hs:
            pref[h] = x0[h] + dx[h][:CH] + d[h]
            p_out[rs, h * hd:(h + 1) * hd] = (p[h] + dx[h][CH:, :hd]).astype(BF16)
            n_out[rs, h * hd:(h + 1) * hd] = n[h] + dx[h][CH:, hd:]
        return carry

    lax.fori_loop(0, nc, chunk, 0)
    x_out[...] = pref[...].astype(BF16)

    def drain(c, carry):
        for kind in range(9):
            transfer(kind, c).wait_send()
        return carry

    lax.fori_loop(0, nc, drain, 0)


def scan_kernel(p_in, n_in, x_in, w0, gain, normed, maps, pairs, quads, prefix, totals, wst, rsend, rrecv, lsend, lrecv, xsend, xrecv):
    heads, hd = x_in.shape[0], x_in.shape[1]
    me = lax.axis_index("ctx")
    z = lax.rem(me, Z)
    x = me // Z
    base = x * Z
    right = base + lax.rem(z + 1, Z)
    left = base + lax.rem(z + Z - 1, Z)

    barrier = pltpu.get_barrier_semaphore()
    for peer in (right, left):
        pl.semaphore_signal(barrier, inc=1, device_id={"ctx": peer}, device_id_type=MESH)
    for d in range(1, X):
        pl.semaphore_signal(
            barrier, inc=1, device_id={"ctx": lax.rem(me + d * Z, X * Z)}, device_id_type=MESH
        )
    maps[z] = x_in[...]
    pl.semaphore_wait(barrier, 2 + X - 1)

    def slot(distance):
        return lax.rem(z + distance + Z, Z)

    reach = {"r": (4, 3), "l": (3, 4)}

    def hop(way, h, s, arriving):
        sign = -1 if way == "r" else 1
        ref = maps.at[slot(sign * (s + 1 if arriving else s)), h]
        ss, rr = (rsend, rrecv) if way == "r" else (lsend, lrecv)
        return pltpu.make_async_remote_copy(
            src_ref=ref, dst_ref=ref, send_sem=ss.at[h, s], recv_sem=rr.at[h, s],
            device_id={"ctx": right if way == "r" else left}, device_id_type=MESH,
        )

    for s in range(4):
        for h in range(heads):
            for way in ("r", "l"):
                if s < reach[way][h]:
                    if s > 0:
                        hop(way, h, s - 1, True).wait_recv()
                    hop(way, h, s, False).start()

    def to_group(h, d):
        ref = totals.at[x, h]
        return pltpu.make_async_remote_copy(
            src_ref=ref, dst_ref=ref, send_sem=xsend.at[h, d - 1], recv_sem=xrecv.at[h, x],
            device_id={"ctx": lax.rem(me + d * Z, X * Z)}, device_id_type=MESH,
        )

    def from_group(h, j):
        ref = totals.at[j, h]
        return pltpu.make_async_remote_copy(
            src_ref=ref, dst_ref=ref, send_sem=xsend.at[h, 0], recv_sem=xrecv.at[h, j],
            device_id={"ctx": me}, device_id_type=MESH,
        )

    for h in range(heads):
        for way in ("r", "l"):
            hop(way, h, reach[way][h] - 1, True).wait_recv()
        ms = [maps[j, h].astype(F32) for j in range(Z)]
        pr = [compose(ms[2 * j + 1], ms[2 * j], hd) for j in range(Z // 2)]
        qd = [compose(pr[2 * j + 1], pr[2 * j], hd) for j in range(Z // 4)]
        totals[x, h] = compose(qd[1], qd[0], hd).astype(BF16)
        for d in range(1, X):
            @pl.when(x + d < X)
            def _():
                to_group(h, d).start()
        for j in range(Z // 2):
            pairs[h, j] = pr[j]
        quads[h] = qd[0]

    for h in range(heads):
        prefix[h] = jnp.zeros_like(prefix[h])

        @pl.when(z >= 4)
        def _():
            prefix[h] = quads[h]

        @pl.when(lax.rem(z, 4) >= 2)
        def _():
            prefix[h] = compose(pairs[h, z // 2 - 1], prefix[h], hd)

        @pl.when(lax.rem(z, 2) == 1)
        def _():
            prefix[h] = compose(maps[z - 1, h].astype(F32), prefix[h], hd)

        wst[h] = w0[h]
        for j in range(X - 1):
            @pl.when(j < x)
            def _():
                from_group(h, j).wait_recv()
                wst[h] = apply_map(totals[j, h].astype(F32), wst[h], hd)

        w = apply_map(prefix[h], wst[h], hd)
        hc = slice(h * hd, (h + 1) * hd)
        zv = dot(p_in[:, hc], w) + n_in[:, hc]
        zv = zv * lax.rsqrt(jnp.mean(zv * zv, -1, keepdims=True) + 1e-06) * gain[h:h + 1, :]
        normed[:, hc] = zv.astype(BF16)

    for h in range(heads):
        for way in ("r", "l"):
            for s in range(reach[way][h]):
                hop(way, h, s, False).wait_send()
        for d in range(1, X):
            @pl.when(x + d < X)
            def _():
                to_group(h, d).wait_send()


def any_spec():
    return pl.BlockSpec(memory_space=pl.ANY)


def vmem_spec():
    return pl.BlockSpec(memory_space=pltpu.VMEM)


def gather_call(hidden_in, w_qkv, lr_weight, inner_lr):
    rows, feat = hidden_in.shape
    _, depth, width = w_qkv.shape
    heads = inner_lr.shape[0]
    hd = width // heads
    nc = rows // CH
    return pl.pallas_call(
        gather_kernel,
        out_shape=(
            jax.ShapeDtypeStruct((rows, width), BF16),
            jax.ShapeDtypeStruct((rows, width), F32),
            jax.ShapeDtypeStruct((heads, hd, 2 * hd), BF16),
        ),
        in_specs=[any_spec(), any_spec(), vmem_spec(), pl.BlockSpec(memory_space=pltpu.SMEM)],
        out_specs=(vmem_spec(), vmem_spec(), vmem_spec()),
        scratch_shapes=[
            pltpu.VMEM((rows, depth), BF16),
            pltpu.VMEM((depth, 3 * width + CH), BF16),
            pltpu.VMEM((CH, depth), F32),
            pltpu.VMEM((heads, hd, 2 * hd), F32),
            pltpu.SemaphoreType.DMA,
            pltpu.SemaphoreType.DMA((nc, 9)),
            pltpu.SemaphoreType.DMA((nc, 9)),
            pltpu.SemaphoreType.DMA((3,)),
        ],
        compiler_params=pltpu.CompilerParams(
            collective_id=0, has_side_effects=True, vmem_limit_bytes=48 * 1024 * 1024
        ),
        name="gather_maps",
    )(hidden_in, w_qkv, lr_weight.T, inner_lr)


def scan_call(p, n, x, init_state, norm_gain):
    rows, width = p.shape
    heads, hd = norm_gain.shape
    return pl.pallas_call(
        scan_kernel,
        out_shape=jax.ShapeDtypeStruct((rows, width), BF16),
        in_specs=[vmem_spec()] * 5,
        out_specs=vmem_spec(),
        scratch_shapes=[
            pltpu.VMEM((Z, heads, hd, 2 * hd), BF16),
            pltpu.VMEM((heads, Z // 2, hd, 2 * hd), F32),
            pltpu.VMEM((heads, hd, 2 * hd), F32),
            pltpu.VMEM((heads, hd, 2 * hd), F32),
            pltpu.VMEM((X, heads, hd, 2 * hd), BF16),
            pltpu.VMEM((heads, hd, hd), F32),
            pltpu.SemaphoreType.DMA((heads, 4)),
            pltpu.SemaphoreType.DMA((heads, 4)),
            pltpu.SemaphoreType.DMA((heads, 4)),
            pltpu.SemaphoreType.DMA((heads, 4)),
            pltpu.SemaphoreType.DMA((heads, X - 1)),
            pltpu.SemaphoreType.DMA((heads, X)),
        ],
        compiler_params=pltpu.CompilerParams(
            collective_id=1, has_side_effects=True, vmem_limit_bytes=48 * 1024 * 1024
        ),
        name="scan_groups",
    )(p, n, x, init_state, norm_gain)


def local(hidden_in, w_qkv, lr_weight, inner_lr, init_state, norm_gain, w_out):
    tp, ctx = lax.axis_size("tp"), lax.axis_size("ctx")
    share = w_out.shape[0] // ctx
    mine = lax.dynamic_slice_in_dim(w_out, lax.axis_index("ctx") * share, share, 0)
    mine = lax.all_to_all(mine, "tp", split_axis=1, concat_axis=0, tiled=True)
    whole = lax.all_gather(mine, "ctx", axis=0, tiled=True)
    whole = whole.reshape(ctx, tp, share, -1).transpose(1, 0, 2, 3).reshape(ctx * tp * share, -1)
    p, n, x = gather_call(hidden_in, w_qkv, lr_weight, inner_lr)
    normed = scan_call(p, n, x, init_state, norm_gain)
    normed = lax.all_gather(normed, "tp", axis=1, tiled=True)
    return jnp.dot(normed, whole, preferred_element_type=F32).astype(BF16)


def solution(mesh):
    in_specs = (
        P("ctx", "tp"),
        P(None, None, "tp"),
        P(None, "tp"),
        P("tp"),
        P("tp", None, None),
        P("tp", None),
        P("tp", None),
    )
    out_specs = P("ctx", "tp")
    return jax.shard_map(local, mesh=mesh, in_specs=in_specs, out_specs=out_specs, check_vma=False)
```

```python
import jax
import jax.numpy as jnp
from jax import lax
from jax.experimental import pallas as pl
from jax.experimental.pallas import tpu as pltpu
from jax.sharding import PartitionSpec as P

MB = 16
CH = 128
MESH = pl.DeviceIdType.MESH
F32 = jnp.float32
BF16 = jnp.bfloat16
Y, CORES = 4, 2
X, Z = 4, 8
TP = Y * CORES


def dot(a, b):
    return jnp.dot(a.astype(BF16), b.astype(BF16), preferred_element_type=F32)


def compose(later, earlier, hd):
    return earlier + dot(later[:, :hd], earlier) + later


def apply_map(m, w, hd):
    return w + dot(m[:, :hd], w) + m[:, hd:]


def pair_gather(src, buf, width, span, me, send, recv):
    half = span // 2
    sib = me + 1 - 2 * lax.rem(me, 2)
    up, down, far = lax.rem(me + 2, TP), lax.rem(me + TP - 2, TP), lax.rem(me + 4, TP)
    sup, sdown, sfar = lax.rem(sib + 2, TP), lax.rem(sib + TP - 2, TP), lax.rem(sib + 4, TP)
    target = (up, down, sib, up, down, sib, sib, sib, sib)
    leaving = (me, me, me, down, up, down, up, far, far)
    landing = (down, up, sib, far, far, sdown, sup, sfar, sfar)

    def place(ref, kind, c, owner):
        r0 = half if kind in (4, 8) else 0
        n = half if kind in (3, 4, 7, 8) else span
        rs = pl.ds(pl.multiple_of(c * span + r0, 16), n)
        if owner is None:
            return ref.at[rs]
        return ref.at[rs, pl.ds(pl.multiple_of(owner * width, width), width)]

    def out(kind, c):
        own = src is not None and kind < 3
        return pltpu.make_async_remote_copy(
            src_ref=place(src, kind, c, None) if own else place(buf, kind, c, leaving[kind]),
            dst_ref=place(buf, kind, c, leaving[kind]),
            send_sem=send.at[c, kind],
            recv_sem=recv.at[c, kind],
            device_id={"tp": target[kind]},
            device_id_type=MESH,
        )

    def arrived(kind, c):
        ref = place(buf, kind, c, landing[kind])
        pltpu.make_async_remote_copy(
            src_ref=ref, dst_ref=ref, send_sem=send.at[c, kind], recv_sem=recv.at[c, kind],
            device_id={"tp": sib}, device_id_type=MESH,
        ).wait_recv()

    def begin(c):
        out(0, c).start()
        out(1, c).start()

    def share(c):
        out(2, c).start()

    def forward(c):
        arrived(0, c)
        out(3, c).start()
        out(5, c).start()
        arrived(1, c)
        out(4, c).start()
        out(6, c).start()

    def far_forward(c):
        arrived(3, c)
        out(7, c).start()
        arrived(4, c)
        out(8, c).start()

    def sent(c):
        for kind in range(9):
            out(kind, c).wait_send()

    return begin, share, forward, far_forward, arrived, sent


def layer_kernel(hid, wq, lrw, lr, w0, gain, wout, mixed,
                 xg, wbuf, lrt, acc, pref, pbuf, nbuf, xbf, mbuf, tbuf, wst, wob, win, ng, wc,
                 loc, wsem, gsend, grecv, asend, arecv, msend, mrecv, tsend, trecv, osend, orecv, hsend, hrecv):
    rows, feat = hid.shape
    nc = rows // CH
    heads, hd = pref.shape[0], pref.shape[1]
    hs = range(heads)
    width = heads * hd
    ocols = mixed.shape[1]
    me = lax.axis_index("tp")
    ctx = lax.axis_index("ctx")
    core = lax.rem(me, 2)
    chip = me // 2
    z = lax.rem(ctx, Z)
    x = ctx // Z
    base = x * Z

    barrier = pltpu.get_barrier_semaphore()
    for t in range(1, TP):
        pl.semaphore_signal(barrier, inc=1, device_id={"tp": lax.rem(me + t, TP)}, device_id_type=MESH)
    for t in range(1, Z):
        pl.semaphore_signal(barrier, inc=1, device_id={"ctx": base + lax.rem(z + t, Z)}, device_id_type=MESH)
    for t in range(1, X):
        pl.semaphore_signal(barrier, inc=1, device_id={"ctx": lax.rem(ctx + t * Z, X * Z)}, device_id_type=MESH)

    wcopies = [pltpu.make_async_copy(wq.at[c], wbuf.at[:, pl.ds(c * width, width)], wsem.at[c]) for c in range(3)]
    for cp in wcopies:
        cp.start()
    own = pltpu.make_async_copy(hid, xg.at[:, pl.ds(pl.multiple_of(me * feat, feat), feat)], loc.at[0])
    own.start()

    def wout_cols(j):
        return wout.at[:, pl.ds(pl.multiple_of(j * ocols, ocols), ocols)]

    def wc_rows(j):
        return wc.at[pl.ds(pl.multiple_of(j * width, width), width)]

    wown = pltpu.make_async_copy(wout_cols(me), wc_rows(me), loc.at[1])
    wown.start()
    begin, share, forward, far_forward, arrived, sent = pair_gather(hid, xg, feat, CH, me, gsend, grecv)
    pl.semaphore_wait(barrier, TP + Z + X - 3)
    begin(0)
    begin(1)
    for c in range(nc):
        share(c)

    lrt[...] = jnp.zeros_like(lrt)
    lrt[0:heads, :] = lrw[...].astype(F32)

    def gate(i, carry):
        at = pl.ds(pl.multiple_of(i * CH, CH), CH)
        wbuf[at, 3 * width:] = lrt[:, at].T.astype(BF16)
        return carry

    lax.fori_loop(0, wbuf.shape[0] // CH, gate, 0)
    pref[...] = jnp.zeros_like(pref)
    own.wait()
    for cp in wcopies:
        cp.wait()

    def part(c, q):
        rs = pl.ds(pl.multiple_of(c * CH, CH), CH)
        ks = pl.ds(pl.multiple_of(lax.rem(chip + q, Y) * 2 * feat, 2 * feat), 2 * feat)
        return jnp.dot(xg[rs, ks], wbuf[ks, :], preferred_element_type=F32)

    def near(c, carry):
        arrived(2, c)
        acc[pl.ds(pl.multiple_of(c * CH, CH), CH), :] = part(c, 0)
        return carry

    def sides(c):
        arrived(5, c)
        arrived(6, c)
        acc[pl.ds(pl.multiple_of(c * CH, CH), CH), :] += part(c, 1) + part(c, Y - 1)

    lax.fori_loop(0, nc, near, 0)
    forward(0)
    begin(2)
    sides(0)
    forward(1)
    begin(3)
    far_forward(0)
    sides(1)

    row = lax.broadcasted_iota(jnp.int32, (CH, CH), 0)
    col = lax.broadcasted_iota(jnp.int32, (CH, CH), 1)
    causal = row >= col
    before = (row >> 4) > (col >> 4)

    def chunk(c, carry):
        arrived(7, c)
        arrived(8, c)
        rs = pl.ds(pl.multiple_of(c * CH, CH), CH)
        proj = acc[rs, :] + part(c, 2)
        part3 = [[proj[:, (k * heads + h) * hd:(k * heads + h + 1) * hd] for h in hs] for k in range(3)]

        def unit(v):
            return v * lax.rsqrt(jnp.sum(v * v, -1, keepdims=True) + hd * 1e-06)

        q = [unit(part3[0][h]) for h in hs]
        k = [unit(part3[1][h]) for h in hs]
        rate = [lr[h] * jax.nn.sigmoid(proj[:, 3 * width + h:3 * width + h + 1]) for h in hs]
        krt = [(k[h] * rate[h]).T.astype(BF16) for h in hs]
        sg = [dot(jnp.concatenate([q[h], k[h]], 0), krt[h]) for h in hs]
        m = [jnp.where(causal, sg[h][:CH], 0.0).astype(BF16) for h in hs]
        l1 = [jnp.where(before, sg[h][CH:], 0.0) for h in hs]
        lb = [l1[h].astype(BF16) for h in hs]
        l2 = [dot(lb[h], lb[h]) for h in hs]
        l34 = [dot(jnp.concatenate([lb[h], l2[h].astype(BF16)], 0), l2[h]) for h in hs]
        t1 = [l2[h] - l1[h] - l34[h][:CH] for h in hs]
        t = [t1[h] + l34[h][CH:] + dot(t1[h], l34[h][CH:]) for h in hs]
        kv = [jnp.concatenate([k[h], part3[2][h]], 1) for h in hs]
        uy = [kv[h] + dot(t[h], kv[h]) for h in hs]
        dn = [dot(jnp.concatenate([krt[h], m[h]], 0), uy[h]) for h in hs]
        d = [jnp.concatenate([-dn[h][:CH, :hd], dn[h][:CH, hd:]], 1) for h in hs]
        p = [q[h] - dn[h][CH:, :hd] for h in hs]
        n = [dn[h][CH:, hd:] for h in hs]
        x0 = [pref[h] for h in hs]
        dx = [dot(jnp.concatenate([d[h][:, :hd], p[h]], 0), x0[h]) for h in hs]
        for h in hs:
            pref[h] = x0[h] + dx[h][:CH] + d[h]
            pbuf[rs, h * hd:(h + 1) * hd] = (p[h] + dx[h][CH:, :hd]).astype(BF16)
            nbuf[rs, h * hd:(h + 1) * hd] = n[h] + dx[h][CH:, hd:]

        @pl.when(c < nc - 2)
        def _():
            forward(c + 2)

        @pl.when(c < nc - 1)
        def _():
            far_forward(c + 1)

        @pl.when(c < nc - 2)
        def _():
            sides(c + 2)

        return carry

    lax.fori_loop(0, nc, chunk, 0)

    def root(h):
        return 4 * core + 2 * h

    def to_root(h):
        return pltpu.make_async_remote_copy(
            src_ref=xbf.at[h], dst_ref=mbuf.at[z], send_sem=msend.at[h], recv_sem=mrecv.at[z],
            device_id={"ctx": base + root(h)}, device_id_type=MESH,
        )

    for h in hs:
        xbf[h] = pref[h].astype(BF16)

        @pl.when(z != root(h))
        def _():
            to_root(h).start()

        @pl.when(z == root(h))
        def _():
            mbuf[z] = xbf[h]

    def to_column(t):
        j = lax.rem(me + t, TP)
        return pltpu.make_async_remote_copy(
            src_ref=wout_cols(j), dst_ref=wc_rows(me), send_sem=asend.at[t - 1], recv_sem=arecv.at[t - 1],
            device_id={"tp": j}, device_id_type=MESH,
        )

    def from_column(t):
        ref = wc_rows(lax.rem(me + TP - t, TP))
        return pltpu.make_async_remote_copy(
            src_ref=ref, dst_ref=ref, send_sem=asend.at[t - 1], recv_sem=arecv.at[t - 1],
            device_id={"tp": lax.rem(me + t, TP)}, device_id_type=MESH,
        )

    for t in range(1, TP):
        to_column(t).start()

    def to_group(d):
        return pltpu.make_async_remote_copy(
            src_ref=tbuf.at[x], dst_ref=tbuf.at[x], send_sem=tsend.at[d - 1], recv_sem=trecv.at[x],
            device_id={"ctx": lax.rem(ctx + d * Z, X * Z)}, device_id_type=MESH,
        )

    def to_member(h, j):
        return pltpu.make_async_remote_copy(
            src_ref=wob.at[j], dst_ref=win.at[h], send_sem=osend.at[j], recv_sem=orecv.at[h],
            device_id={"ctx": base + j}, device_id_type=MESH,
        )

    is_root = (z == root(0)) | (z == root(1))
    mine = lax.rem(z, 4) // 2

    @pl.when(is_root)
    def _():
        for j in range(Z):
            @pl.when(z != j)
            def _():
                pltpu.make_async_remote_copy(
                    src_ref=mbuf.at[j], dst_ref=mbuf.at[j], send_sem=msend.at[0], recv_sem=mrecv.at[j],
                    device_id={"ctx": base + lax.rem(z + 1, Z)}, device_id_type=MESH,
                ).wait_recv()
        ms = [mbuf[j].astype(F32) for j in range(Z)]
        pr = [compose(ms[2 * j + 1], ms[2 * j], hd) for j in range(Z // 2)]
        qd = [compose(pr[2 * j + 1], pr[2 * j], hd) for j in range(Z // 4)]
        tbuf[x] = compose(qd[1], qd[0], hd).astype(BF16)
        for d in range(1, X):
            @pl.when(x + d < X)
            def _():
                to_group(d).start()
        six = compose(pr[2], qd[0], hd)
        pre = [None, ms[0], pr[0], compose(ms[2], pr[0], hd), qd[0], compose(ms[4], qd[0], hd), six,
               compose(ms[6], six, hd)]
        wst[...] = w0[mine]
        for j in range(X - 1):
            @pl.when(j < x)
            def _():
                pltpu.make_async_remote_copy(
                    src_ref=tbuf.at[j], dst_ref=tbuf.at[j], send_sem=tsend.at[0], recv_sem=trecv.at[j],
                    device_id={"ctx": lax.rem(ctx + Z, X * Z)}, device_id_type=MESH,
                ).wait_recv()
                wst[...] = apply_map(tbuf[j].astype(F32), wst[...], hd)
        w = wst[...]
        for j in range(Z):
            wob[j] = (w if j == 0 else apply_map(pre[j], w, hd)).astype(BF16)
        for j in range(Z):
            @pl.when(z != j)
            def _():
                to_member(mine, j).start()
        win[mine] = wob[z]

    gbegin, gshare, gforward, gfar_forward, garrived, gsent = pair_gather(
        None, ng, width, rows // 2, me, hsend, hrecv)
    for h in hs:
        @pl.when(z != root(h))
        def _():
            pltpu.make_async_remote_copy(
                src_ref=win.at[h], dst_ref=win.at[h], send_sem=osend.at[0], recv_sem=orecv.at[h],
                device_id={"ctx": base + lax.rem(z + 1, Z)}, device_id_type=MESH,
            ).wait_recv()
    for c in range(2):
        rs = slice(c * (rows // 2), (c + 1) * (rows // 2))
        for h in hs:
            hc = slice(h * hd, (h + 1) * hd)
            zv = dot(pbuf[rs, hc], win[h]) + nbuf[rs, hc]
            zv = zv * lax.rsqrt(jnp.mean(zv * zv, -1, keepdims=True) + 1e-06) * gain[h:h + 1, :]
            ng[rs, pl.ds(pl.multiple_of(me * width + h * hd, hd), hd)] = zv.astype(BF16)
        gbegin(c)
        gshare(c)
    for c in range(2):
        gforward(c)
    for t in range(1, TP):
        from_column(t).wait_recv()
    wown.wait()
    for c in range(2):
        gfar_forward(c)
    for c in range(2):
        for kind in (2, 5, 6, 7, 8):
            garrived(kind, c)
        rs = slice(c * (rows // 2), (c + 1) * (rows // 2))
        mixed[rs, :] = jnp.dot(ng[rs, :], wc[...], preferred_element_type=F32).astype(BF16)

    def drain(c, carry):
        sent(c)
        return carry

    lax.fori_loop(0, nc, drain, 0)
    for c in range(2):
        gsent(c)
    for t in range(1, TP):
        to_column(t).wait_send()
    for h in hs:
        @pl.when(z != root(h))
        def _():
            to_root(h).wait_send()

    @pl.when(is_root)
    def _():
        for d in range(1, X):
            @pl.when(x + d < X)
            def _():
                to_group(d).wait_send()
        for j in range(Z):
            @pl.when(z != j)
            def _():
                to_member(mine, j).wait_send()


def any_spec():
    return pl.BlockSpec(memory_space=pl.ANY)


def vmem_spec():
    return pl.BlockSpec(memory_space=pltpu.VMEM)


def local(hidden_in, w_qkv, lr_weight, inner_lr, init_state, norm_gain, w_out):
    rows, feat = hidden_in.shape
    _, depth, width = w_qkv.shape
    heads, hd = norm_gain.shape
    nc = rows // CH
    out_cols = w_out.shape[1] // TP
    dma = pltpu.SemaphoreType.DMA
    return pl.pallas_call(
        layer_kernel,
        out_shape=jax.ShapeDtypeStruct((rows, out_cols), BF16),
        in_specs=[any_spec(), any_spec(), vmem_spec(), pl.BlockSpec(memory_space=pltpu.SMEM),
                  vmem_spec(), vmem_spec(), any_spec()],
        out_specs=vmem_spec(),
        scratch_shapes=[
            pltpu.VMEM((rows, depth), BF16),
            pltpu.VMEM((depth, 3 * width + CH), BF16),
            pltpu.VMEM((CH, depth), F32),
            pltpu.VMEM((rows, 3 * width + CH), F32),
            pltpu.VMEM((heads, hd, 2 * hd), F32),
            pltpu.VMEM((rows, width), BF16),
            pltpu.VMEM((rows, width), F32),
            pltpu.VMEM((heads, hd, 2 * hd), BF16),
            pltpu.VMEM((Z, hd, 2 * hd), BF16),
            pltpu.VMEM((X, hd, 2 * hd), BF16),
            pltpu.VMEM((hd, hd), F32),
            pltpu.VMEM((Z, hd, hd), BF16),
            pltpu.VMEM((heads, hd, hd), BF16),
            pltpu.VMEM((rows, TP * width), BF16),
            pltpu.VMEM((TP * width, out_cols), BF16),
            dma((2,)),
            dma((3,)),
            dma((nc, 9)),
            dma((nc, 9)),
            dma((TP - 1,)),
            dma((TP - 1,)),
            dma((heads,)),
            dma((Z,)),
            dma((X - 1,)),
            dma((X,)),
            dma((Z,)),
            dma((heads,)),
            dma((2, 9)),
            dma((2, 9)),
        ],
        compiler_params=pltpu.CompilerParams(
            collective_id=0, has_side_effects=True, vmem_limit_bytes=48 * 1024 * 1024
        ),
        name="layer",
    )(hidden_in, w_qkv, lr_weight.T, inner_lr, init_state, norm_gain, w_out)


def solution(mesh):
    in_specs = (
        P("ctx", "tp"),
        P(None, None, "tp"),
        P(None, "tp"),
        P("tp"),
        P("tp", None, None),
        P("tp", None),
        P("tp", None),
    )
    out_specs = P("ctx", "tp")
    return jax.shard_map(local, mesh=mesh, in_specs=in_specs, out_specs=out_specs, check_vma=False)
```

```python
import jax
import jax.numpy as jnp
from jax import lax
from jax.experimental import pallas as pl
from jax.experimental.pallas import tpu as pltpu
from jax.sharding import PartitionSpec as P

MB = 16
CH = 128
MESH = pl.DeviceIdType.MESH
F32 = jnp.float32
BF16 = jnp.bfloat16
Y, CORES = 4, 2
X, Z = 4, 8
TP = Y * CORES


def dot(a, b):
    return jnp.dot(a.astype(BF16), b.astype(BF16), preferred_element_type=F32)


def compose(later, earlier, hd):
    return earlier + dot(later[:, :hd], earlier) + later


def apply_map(m, w, hd):
    return w + dot(m[:, :hd], w) + m[:, hd:]


def pair_gather(src, buf, width, span, me, send, recv):
    half = span // 2
    sib = me + 1 - 2 * lax.rem(me, 2)
    up, down, far = lax.rem(me + 2, TP), lax.rem(me + TP - 2, TP), lax.rem(me + 4, TP)
    sup, sdown, sfar = lax.rem(sib + 2, TP), lax.rem(sib + TP - 2, TP), lax.rem(sib + 4, TP)
    target = (up, down, sib, up, down, sib, sib, sib, sib)
    leaving = (me, me, me, down, up, down, up, far, far)
    landing = (down, up, sib, far, far, sdown, sup, sfar, sfar)

    def place(ref, kind, c, owner):
        r0 = half if kind in (4, 8) else 0
        n = half if kind in (3, 4, 7, 8) else span
        rs = pl.ds(pl.multiple_of(c * span + r0, 16), n)
        if owner is None:
            return ref.at[rs]
        return ref.at[rs, pl.ds(pl.multiple_of(owner * width, width), width)]

    def out(kind, c):
        own = src is not None and kind < 3
        return pltpu.make_async_remote_copy(
            src_ref=place(src, kind, c, None) if own else place(buf, kind, c, leaving[kind]),
            dst_ref=place(buf, kind, c, leaving[kind]),
            send_sem=send.at[c, kind],
            recv_sem=recv.at[c, kind],
            device_id={"tp": target[kind]},
            device_id_type=MESH,
        )

    def arrived(kind, c):
        ref = place(buf, kind, c, landing[kind])
        pltpu.make_async_remote_copy(
            src_ref=ref, dst_ref=ref, send_sem=send.at[c, kind], recv_sem=recv.at[c, kind],
            device_id={"tp": sib}, device_id_type=MESH,
        ).wait_recv()

    def begin(c):
        out(0, c).start()
        out(1, c).start()

    def share(c):
        out(2, c).start()

    def forward(c):
        arrived(0, c)
        out(3, c).start()
        out(5, c).start()
        arrived(1, c)
        out(4, c).start()
        out(6, c).start()

    def far_forward(c):
        arrived(3, c)
        out(7, c).start()
        arrived(4, c)
        out(8, c).start()

    def sent(c):
        for kind in range(9):
            out(kind, c).wait_send()

    return begin, share, forward, far_forward, arrived, sent


def layer_kernel(hid, wq, lrw_in, lr_in, w0_in, gain_in, wout, mixed,
                 lrw, lr, w0, gain, xg, wbuf, lrt, acc, pref, pbuf, nbuf, xbf, mbuf, tbuf, wst, wob, win, ng, wc,
                 loc, lsem, wsem, gsend, grecv, asend, arecv, msend, mrecv, tsend, trecv, osend, orecv, hsend, hrecv):
    rows, feat = hid.shape
    nc = rows // CH
    heads, hd = pref.shape[0], pref.shape[1]
    hs = range(heads)
    width = heads * hd
    ocols = mixed.shape[1]
    me = lax.axis_index("tp")
    ctx = lax.axis_index("ctx")
    core = lax.rem(me, 2)
    chip = me // 2
    z = lax.rem(ctx, Z)
    x = ctx // Z
    base = x * Z

    smalls = [
        pltpu.make_async_copy(a, b, lsem.at[i])
        for i, (a, b) in enumerate(((lrw_in, lrw), (lr_in, lr), (w0_in, w0), (gain_in, gain)))
    ]
    for cp in smalls:
        cp.start()
    barrier = pltpu.get_barrier_semaphore()
    for t in range(1, TP):
        pl.semaphore_signal(barrier, inc=1, device_id={"tp": lax.rem(me + t, TP)}, device_id_type=MESH)
    for t in range(1, Z):
        pl.semaphore_signal(barrier, inc=1, device_id={"ctx": base + lax.rem(z + t, Z)}, device_id_type=MESH)
    for t in range(1, X):
        pl.semaphore_signal(barrier, inc=1, device_id={"ctx": lax.rem(ctx + t * Z, X * Z)}, device_id_type=MESH)

    wcopies = [pltpu.make_async_copy(wq.at[c], wbuf.at[:, pl.ds(c * width, width)], wsem.at[c]) for c in range(3)]
    for cp in wcopies:
        cp.start()
    own = pltpu.make_async_copy(hid, xg.at[:, pl.ds(pl.multiple_of(me * feat, feat), feat)], loc.at[0])
    own.start()

    def wout_cols(j):
        return wout.at[:, pl.ds(pl.multiple_of(j * ocols, ocols), ocols)]

    def wc_rows(j):
        return wc.at[pl.ds(pl.multiple_of(j * width, width), width)]

    wown = pltpu.make_async_copy(wout_cols(me), wc_rows(me), loc.at[1])
    wown.start()
    begin, share, forward, far_forward, arrived, sent = pair_gather(hid, xg, feat, CH, me, gsend, grecv)
    pl.semaphore_wait(barrier, TP + Z + X - 3)
    begin(0)
    begin(1)
    for c in range(nc):
        share(c)

    lrt[...] = jnp.zeros_like(lrt)
    for cp in smalls:
        cp.wait()
    lrt[0:heads, :] = lrw[...].astype(F32)

    def gate(i, carry):
        at = pl.ds(pl.multiple_of(i * CH, CH), CH)
        wbuf[at, 3 * width:] = lrt[:, at].T.astype(BF16)
        return carry

    lax.fori_loop(0, wbuf.shape[0] // CH, gate, 0)
    pref[...] = jnp.zeros_like(pref)
    own.wait()
    for cp in wcopies:
        cp.wait()

    def to_column(t):
        j = lax.rem(me + t, TP)
        return pltpu.make_async_remote_copy(
            src_ref=wout_cols(j), dst_ref=wc_rows(me), send_sem=asend.at[t - 1], recv_sem=arecv.at[t - 1],
            device_id={"tp": j}, device_id_type=MESH,
        )

    def from_column(t):
        ref = wc_rows(lax.rem(me + TP - t, TP))
        return pltpu.make_async_remote_copy(
            src_ref=ref, dst_ref=ref, send_sem=asend.at[t - 1], recv_sem=arecv.at[t - 1],
            device_id={"tp": lax.rem(me + t, TP)}, device_id_type=MESH,
        )

    def part(c, q):
        rs = pl.ds(pl.multiple_of(c * CH, CH), CH)
        ks = pl.ds(pl.multiple_of(lax.rem(chip + q, Y) * 2 * feat, 2 * feat), 2 * feat)
        return jnp.dot(xg[rs, ks], wbuf[ks, :], preferred_element_type=F32)

    def near(c, carry):
        arrived(2, c)
        acc[pl.ds(pl.multiple_of(c * CH, CH), CH), :] = part(c, 0)
        return carry

    def sides(c):
        arrived(5, c)
        arrived(6, c)
        acc[pl.ds(pl.multiple_of(c * CH, CH), CH), :] += part(c, 1) + part(c, Y - 1)

    lax.fori_loop(0, nc, near, 0)
    forward(0)
    begin(2)
    sides(0)
    forward(1)
    begin(3)
    far_forward(0)
    sides(1)

    row = lax.broadcasted_iota(jnp.int32, (CH, CH), 0)
    col = lax.broadcasted_iota(jnp.int32, (CH, CH), 1)
    causal = row >= col
    before = (row >> 4) > (col >> 4)

    def chunk(c, carry):
        arrived(7, c)
        arrived(8, c)
        rs = pl.ds(pl.multiple_of(c * CH, CH), CH)
        proj = acc[rs, :] + part(c, 2)
        part3 = [[proj[:, (k * heads + h) * hd:(k * heads + h + 1) * hd] for h in hs] for k in range(3)]

        def unit(v):
            return v * lax.rsqrt(jnp.sum(v * v, -1, keepdims=True) + hd * 1e-06)

        q = [unit(part3[0][h]) for h in hs]
        k = [unit(part3[1][h]) for h in hs]
        rate = [lr[h] * jax.nn.sigmoid(proj[:, 3 * width + h:3 * width + h + 1]) for h in hs]
        krt = [(k[h] * rate[h]).T.astype(BF16) for h in hs]
        sg = [dot(jnp.concatenate([q[h], k[h]], 0), krt[h]) for h in hs]
        m = [jnp.where(causal, sg[h][:CH], 0.0).astype(BF16) for h in hs]
        l1 = [jnp.where(before, sg[h][CH:], 0.0) for h in hs]
        lb = [l1[h].astype(BF16) for h in hs]
        l2 = [dot(lb[h], lb[h]) for h in hs]
        l34 = [dot(jnp.concatenate([lb[h], l2[h].astype(BF16)], 0), l2[h]) for h in hs]
        t1 = [l2[h] - l1[h] - l34[h][:CH] for h in hs]
        t = [t1[h] + l34[h][CH:] + dot(t1[h], l34[h][CH:]) for h in hs]
        kv = [jnp.concatenate([k[h], part3[2][h]], 1) for h in hs]
        uy = [kv[h] + dot(t[h], kv[h]) for h in hs]
        dn = [dot(jnp.concatenate([krt[h], m[h]], 0), uy[h]) for h in hs]
        d = [jnp.concatenate([-dn[h][:CH, :hd], dn[h][:CH, hd:]], 1) for h in hs]
        p = [q[h] - dn[h][CH:, :hd] for h in hs]
        n = [dn[h][CH:, hd:] for h in hs]
        x0 = [pref[h] for h in hs]
        dx = [dot(jnp.concatenate([d[h][:, :hd], p[h]], 0), x0[h]) for h in hs]
        for h in hs:
            pref[h] = x0[h] + dx[h][:CH] + d[h]
            pbuf[rs, h * hd:(h + 1) * hd] = (p[h] + dx[h][CH:, :hd]).astype(BF16)
            nbuf[rs, h * hd:(h + 1) * hd] = n[h] + dx[h][CH:, hd:]

        @pl.when(c < nc - 2)
        def _():
            forward(c + 2)

        @pl.when(c < nc - 1)
        def _():
            far_forward(c + 1)

        @pl.when(c == nc - 2)
        def _():
            for t in range(1, TP):
                to_column(t).start()

        @pl.when(c < nc - 2)
        def _():
            sides(c + 2)

        return carry

    lax.fori_loop(0, nc, chunk, 0)

    def root(h):
        return 4 * core + 2 * h

    def to_root(h):
        return pltpu.make_async_remote_copy(
            src_ref=xbf.at[h], dst_ref=mbuf.at[z], send_sem=msend.at[h], recv_sem=mrecv.at[z],
            device_id={"ctx": base + root(h)}, device_id_type=MESH,
        )

    for h in hs:
        xbf[h] = pref[h].astype(BF16)

        @pl.when(z != root(h))
        def _():
            to_root(h).start()

        @pl.when(z == root(h))
        def _():
            mbuf[z] = xbf[h]

    def to_group(d):
        return pltpu.make_async_remote_copy(
            src_ref=tbuf.at[x], dst_ref=tbuf.at[x], send_sem=tsend.at[d - 1], recv_sem=trecv.at[x],
            device_id={"ctx": lax.rem(ctx + d * Z, X * Z)}, device_id_type=MESH,
        )

    def to_member(h, j):
        return pltpu.make_async_remote_copy(
            src_ref=wob.at[j], dst_ref=win.at[h], send_sem=osend.at[j], recv_sem=orecv.at[h],
            device_id={"ctx": base + j}, device_id_type=MESH,
        )

    is_root = (z == root(0)) | (z == root(1))
    mine = lax.rem(z, 4) // 2

    @pl.when(is_root)
    def _():
        for j in range(Z):
            @pl.when(z != j)
            def _():
                pltpu.make_async_remote_copy(
                    src_ref=mbuf.at[j], dst_ref=mbuf.at[j], send_sem=msend.at[0], recv_sem=mrecv.at[j],
                    device_id={"ctx": base + lax.rem(z + 1, Z)}, device_id_type=MESH,
                ).wait_recv()
        ms = [mbuf[j].astype(F32) for j in range(Z)]
        pr = [compose(ms[2 * j + 1], ms[2 * j], hd) for j in range(Z // 2)]
        qd = [compose(pr[2 * j + 1], pr[2 * j], hd) for j in range(Z // 4)]
        tbuf[x] = compose(qd[1], qd[0], hd).astype(BF16)
        for d in range(1, X):
            @pl.when(x + d < X)
            def _():
                to_group(d).start()
        six = compose(pr[2], qd[0], hd)
        pre = [None, ms[0], pr[0], compose(ms[2], pr[0], hd), qd[0], compose(ms[4], qd[0], hd), six,
               compose(ms[6], six, hd)]
        wst[...] = w0[mine]
        for j in range(X - 1):
            @pl.when(j < x)
            def _():
                pltpu.make_async_remote_copy(
                    src_ref=tbuf.at[j], dst_ref=tbuf.at[j], send_sem=tsend.at[0], recv_sem=trecv.at[j],
                    device_id={"ctx": lax.rem(ctx + Z, X * Z)}, device_id_type=MESH,
                ).wait_recv()
                wst[...] = apply_map(tbuf[j].astype(F32), wst[...], hd)
        w = wst[...]
        for j in range(Z):
            wob[j] = (w if j == 0 else apply_map(pre[j], w, hd)).astype(BF16)
        for j in range(Z):
            @pl.when(z != j)
            def _():
                to_member(mine, j).start()
        win[mine] = wob[z]

    gbegin, gshare, gforward, gfar_forward, garrived, gsent = pair_gather(
        None, ng, width, rows // 2, me, hsend, hrecv)
    for h in hs:
        @pl.when(z != root(h))
        def _():
            pltpu.make_async_remote_copy(
                src_ref=win.at[h], dst_ref=win.at[h], send_sem=osend.at[0], recv_sem=orecv.at[h],
                device_id={"ctx": base + lax.rem(z + 1, Z)}, device_id_type=MESH,
            ).wait_recv()
    for c in range(2):
        rs = slice(c * (rows // 2), (c + 1) * (rows // 2))
        for h in hs:
            hc = slice(h * hd, (h + 1) * hd)
            zv = dot(pbuf[rs, hc], win[h]) + nbuf[rs, hc]
            zv = zv * lax.rsqrt(jnp.mean(zv * zv, -1, keepdims=True) + 1e-06) * gain[h:h + 1, :]
            ng[rs, pl.ds(pl.multiple_of(me * width + h * hd, hd), hd)] = zv.astype(BF16)
        gbegin(c)
        gshare(c)
    for c in range(2):
        gforward(c)
    for t in range(1, TP):
        from_column(t).wait_recv()
    wown.wait()
    for c in range(2):
        gfar_forward(c)
    for c in range(2):
        for kind in (2, 5, 6, 7, 8):
            garrived(kind, c)
        rs = slice(c * (rows // 2), (c + 1) * (rows // 2))
        mixed[rs, :] = jnp.dot(ng[rs, :], wc[...], preferred_element_type=F32).astype(BF16)

    def drain(c, carry):
        sent(c)
        return carry

    lax.fori_loop(0, nc, drain, 0)
    for c in range(2):
        gsent(c)
    for t in range(1, TP):
        to_column(t).wait_send()
    for h in hs:
        @pl.when(z != root(h))
        def _():
            to_root(h).wait_send()

    @pl.when(is_root)
    def _():
        for d in range(1, X):
            @pl.when(x + d < X)
            def _():
                to_group(d).wait_send()
        for j in range(Z):
            @pl.when(z != j)
            def _():
                to_member(mine, j).wait_send()


def vmem_spec():
    return pl.BlockSpec(memory_space=pltpu.VMEM)


def local(hidden_in, w_qkv, lr_weight, inner_lr, init_state, norm_gain, w_out):
    rows, feat = hidden_in.shape
    _, depth, width = w_qkv.shape
    heads, hd = norm_gain.shape
    nc = rows // CH
    out_cols = w_out.shape[1] // TP
    dma = pltpu.SemaphoreType.DMA
    return pl.pallas_call(
        layer_kernel,
        out_shape=jax.ShapeDtypeStruct((rows, out_cols), BF16),
        in_specs=[pl.BlockSpec(memory_space=pltpu.HBM)] * 7,
        out_specs=vmem_spec(),
        scratch_shapes=[
            pltpu.VMEM((heads, depth), BF16),
            pltpu.SMEM((heads,), F32),
            pltpu.VMEM((heads, hd, hd), F32),
            pltpu.VMEM((heads, hd), F32),
            pltpu.VMEM((rows, depth), BF16),
            pltpu.VMEM((depth, 3 * width + CH), BF16),
            pltpu.VMEM((CH, depth), F32),
            pltpu.VMEM((rows, 3 * width + CH), F32),
            pltpu.VMEM((heads, hd, 2 * hd), F32),
            pltpu.VMEM((rows, width), BF16),
            pltpu.VMEM((rows, width), F32),
            pltpu.VMEM((heads, hd, 2 * hd), BF16),
            pltpu.VMEM((Z, hd, 2 * hd), BF16),
            pltpu.VMEM((X, hd, 2 * hd), BF16),
            pltpu.VMEM((hd, hd), F32),
            pltpu.VMEM((Z, hd, hd), BF16),
            pltpu.VMEM((heads, hd, hd), BF16),
            pltpu.VMEM((rows, TP * width), BF16),
            pltpu.VMEM((TP * width, out_cols), BF16),
            dma((2,)),
            dma((4,)),
            dma((3,)),
            dma((nc, 9)),
            dma((nc, 9)),
            dma((TP - 1,)),
            dma((TP - 1,)),
            dma((heads,)),
            dma((Z,)),
            dma((X - 1,)),
            dma((X,)),
            dma((Z,)),
            dma((heads,)),
            dma((2, 9)),
            dma((2, 9)),
        ],
        compiler_params=pltpu.CompilerParams(
            collective_id=0, has_side_effects=True, vmem_limit_bytes=48 * 1024 * 1024
        ),
        name="layer",
    )(hidden_in, w_qkv, lr_weight.T, inner_lr, init_state, norm_gain, w_out)


def solution(mesh):
    in_specs = (
        P("ctx", "tp"),
        P(None, None, "tp"),
        P(None, "tp"),
        P("tp"),
        P("tp", None, None),
        P("tp", None),
        P("tp", None),
    )
    out_specs = P("ctx", "tp")
    return jax.shard_map(local, mesh=mesh, in_specs=in_specs, out_specs=out_specs, check_vma=False)
```

```python
import jax
import jax.numpy as jnp
from jax import lax
from jax.experimental import pallas as pl
from jax.experimental.pallas import tpu as pltpu
from jax.sharding import PartitionSpec as P

MB = 16
CH = 128
MESH = pl.DeviceIdType.MESH
F32 = jnp.float32
BF16 = jnp.bfloat16
Y, CORES = 4, 2
X, Z = 4, 8
TP = Y * CORES


def dot(a, b):
    return jnp.dot(a.astype(BF16), b.astype(BF16), preferred_element_type=F32)


def compose(later, earlier, hd):
    return earlier + dot(later[:, :hd], earlier) + later


def apply_map(m, w, hd):
    return w + dot(m[:, :hd], w) + m[:, hd:]


def pair_gather(src, buf, width, span, me, send, recv):
    half = span // 2
    sib = me + 1 - 2 * lax.rem(me, 2)
    up, down, far = lax.rem(me + 2, TP), lax.rem(me + TP - 2, TP), lax.rem(me + 4, TP)
    sup, sdown, sfar = lax.rem(sib + 2, TP), lax.rem(sib + TP - 2, TP), lax.rem(sib + 4, TP)
    target = (up, down, sib, up, down, sib, sib, sib, sib)
    leaving = (me, me, me, down, up, down, up, far, far)
    landing = (down, up, sib, far, far, sdown, sup, sfar, sfar)

    def place(ref, kind, c, owner):
        r0 = half if kind in (4, 8) else 0
        n = half if kind in (3, 4, 7, 8) else span
        rs = pl.ds(pl.multiple_of(c * span + r0, 16), n)
        if owner is None:
            return ref.at[rs]
        return ref.at[rs, pl.ds(pl.multiple_of(owner * width, width), width)]

    def out(kind, c):
        own = src is not None and kind < 3
        return pltpu.make_async_remote_copy(
            src_ref=place(src, kind, c, None) if own else place(buf, kind, c, leaving[kind]),
            dst_ref=place(buf, kind, c, leaving[kind]),
            send_sem=send.at[c, kind],
            recv_sem=recv.at[c, kind],
            device_id={"tp": target[kind]},
            device_id_type=MESH,
        )

    def arrived(kind, c):
        ref = place(buf, kind, c, landing[kind])
        pltpu.make_async_remote_copy(
            src_ref=ref, dst_ref=ref, send_sem=send.at[c, kind], recv_sem=recv.at[c, kind],
            device_id={"tp": sib}, device_id_type=MESH,
        ).wait_recv()

    def begin(c):
        out(0, c).start()
        out(1, c).start()

    def share(c):
        out(2, c).start()

    def forward(c):
        arrived(0, c)
        out(3, c).start()
        out(5, c).start()
        arrived(1, c)
        out(4, c).start()
        out(6, c).start()

    def far_forward(c):
        arrived(3, c)
        out(7, c).start()
        arrived(4, c)
        out(8, c).start()

    def sent(c):
        for kind in range(9):
            out(kind, c).wait_send()

    return begin, share, forward, far_forward, arrived, sent


def layer_kernel(hid, wq, lrw_in, lr_in, w0_in, gain_in, wout, mixed,
                 lrw, lr, w0, gain, xg, wbuf, lrt, acc, pref, pbuf, nbuf, xbf, mbuf, tbuf, wst, wob, win, ng, wc,
                 loc, lsem, wsem, gsend, grecv, asend, arecv, msend, mrecv, tsend, trecv, osend, orecv, hsend, hrecv):
    rows, feat = hid.shape
    nc = rows // CH
    heads, hd = pref.shape[0], pref.shape[1]
    hs = range(heads)
    width = heads * hd
    ocols = mixed.shape[1]
    me = lax.axis_index("tp")
    ctx = lax.axis_index("ctx")
    core = lax.rem(me, 2)
    chip = me // 2
    z = lax.rem(ctx, Z)
    x = ctx // Z
    base = x * Z

    smalls = [
        pltpu.make_async_copy(a, b, lsem.at[i])
        for i, (a, b) in enumerate(((lrw_in, lrw), (lr_in, lr), (w0_in, w0), (gain_in, gain)))
    ]
    for cp in smalls:
        cp.start()
    barrier = pltpu.get_barrier_semaphore()
    for t in range(1, TP):
        pl.semaphore_signal(barrier, inc=1, device_id={"tp": lax.rem(me + t, TP)}, device_id_type=MESH)
    for t in range(1, Z):
        pl.semaphore_signal(barrier, inc=1, device_id={"ctx": base + lax.rem(z + t, Z)}, device_id_type=MESH)
    for t in range(1, X):
        pl.semaphore_signal(barrier, inc=1, device_id={"ctx": lax.rem(ctx + t * Z, X * Z)}, device_id_type=MESH)

    wcopies = [pltpu.make_async_copy(wq.at[c], wbuf.at[:, pl.ds(c * width, width)], wsem.at[c]) for c in range(3)]
    for cp in wcopies:
        cp.start()
    own = pltpu.make_async_copy(hid, xg.at[:, pl.ds(pl.multiple_of(me * feat, feat), feat)], loc.at[0])
    own.start()

    def wout_cols(j):
        return wout.at[:, pl.ds(pl.multiple_of(j * ocols, ocols), ocols)]

    def wc_rows(j):
        return wc.at[pl.ds(pl.multiple_of(j * width, width), width)]

    wown = pltpu.make_async_copy(wout_cols(me), wc_rows(me), loc.at[1])
    wown.start()
    begin, share, forward, far_forward, arrived, sent = pair_gather(hid, xg, feat, CH, me, gsend, grecv)
    pl.semaphore_wait(barrier, TP + Z + X - 3)
    begin(0)
    begin(1)
    for c in range(nc):
        share(c)

    lrt[...] = jnp.zeros_like(lrt)
    for cp in smalls:
        cp.wait()
    lrt[0:heads, :] = lrw[...].astype(F32)

    def gate(i, carry):
        at = pl.ds(pl.multiple_of(i * CH, CH), CH)
        wbuf[at, 3 * width:] = lrt[:, at].T.astype(BF16)
        return carry

    lax.fori_loop(0, wbuf.shape[0] // CH, gate, 0)
    pref[...] = jnp.zeros_like(pref)
    own.wait()
    for cp in wcopies:
        cp.wait()

    def to_column(t):
        j = lax.rem(me + t, TP)
        return pltpu.make_async_remote_copy(
            src_ref=wout_cols(j), dst_ref=wc_rows(me), send_sem=asend.at[t - 1], recv_sem=arecv.at[t - 1],
            device_id={"tp": j}, device_id_type=MESH,
        )

    def from_column(t):
        ref = wc_rows(lax.rem(me + TP - t, TP))
        return pltpu.make_async_remote_copy(
            src_ref=ref, dst_ref=ref, send_sem=asend.at[t - 1], recv_sem=arecv.at[t - 1],
            device_id={"tp": lax.rem(me + t, TP)}, device_id_type=MESH,
        )

    def part(c, q):
        rs = pl.ds(pl.multiple_of(c * CH, CH), CH)
        ks = pl.ds(pl.multiple_of(lax.rem(chip + q, Y) * 2 * feat, 2 * feat), 2 * feat)
        return jnp.dot(xg[rs, ks], wbuf[ks, :], preferred_element_type=F32)

    def near(c, carry):
        arrived(2, c)
        acc[pl.ds(pl.multiple_of(c * CH, CH), CH), :] = part(c, 0)
        return carry

    def sides(c):
        arrived(5, c)
        arrived(6, c)
        acc[pl.ds(pl.multiple_of(c * CH, CH), CH), :] += part(c, 1) + part(c, Y - 1)

    lax.fori_loop(0, nc, near, 0)
    forward(0)
    begin(2)
    sides(0)
    forward(1)
    begin(3)
    far_forward(0)
    sides(1)

    row = lax.broadcasted_iota(jnp.int32, (CH, CH), 0)
    col = lax.broadcasted_iota(jnp.int32, (CH, CH), 1)
    causal = row >= col
    before = (row >> 4) > (col >> 4)

    def chunk(c, carry):
        arrived(7, c)
        arrived(8, c)
        rs = pl.ds(pl.multiple_of(c * CH, CH), CH)
        proj = acc[rs, :] + part(c, 2)
        part3 = [[proj[:, (k * heads + h) * hd:(k * heads + h + 1) * hd] for h in hs] for k in range(3)]

        def unit(v):
            return v * lax.rsqrt(jnp.sum(v * v, -1, keepdims=True) + hd * 1e-06)

        q = [unit(part3[0][h]) for h in hs]
        k = [unit(part3[1][h]) for h in hs]
        rate = [lr[h] * jax.nn.sigmoid(proj[:, 3 * width + h:3 * width + h + 1]) for h in hs]
        krt = [(k[h] * rate[h]).T.astype(BF16) for h in hs]
        sg = [dot(jnp.concatenate([q[h], k[h]], 0), krt[h]) for h in hs]
        m = [jnp.where(causal, sg[h][:CH], 0.0).astype(BF16) for h in hs]
        l1 = [jnp.where(before, sg[h][CH:], 0.0) for h in hs]
        lb = [l1[h].astype(BF16) for h in hs]
        l2 = [dot(lb[h], lb[h]) for h in hs]
        l34 = [dot(jnp.concatenate([lb[h], l2[h].astype(BF16)], 0), l2[h]) for h in hs]
        t1 = [l2[h] - l1[h] - l34[h][:CH] for h in hs]
        t = [t1[h] + l34[h][CH:] + dot(t1[h], l34[h][CH:]) for h in hs]
        kv = [jnp.concatenate([k[h], part3[2][h]], 1) for h in hs]
        uy = [kv[h] + dot(t[h], kv[h]) for h in hs]
        dn = [dot(jnp.concatenate([krt[h], m[h]], 0), uy[h]) for h in hs]
        d = [jnp.concatenate([-dn[h][:CH, :hd], dn[h][:CH, hd:]], 1) for h in hs]
        p = [q[h] - dn[h][CH:, :hd] for h in hs]
        n = [dn[h][CH:, hd:] for h in hs]
        x0 = [pref[h] for h in hs]
        dx = [dot(jnp.concatenate([d[h][:, :hd], p[h]], 0), x0[h]) for h in hs]
        for h in hs:
            pref[h] = x0[h] + dx[h][:CH] + d[h]
            pbuf[rs, h * hd:(h + 1) * hd] = (p[h] + dx[h][CH:, :hd]).astype(BF16)
            nbuf[rs, h * hd:(h + 1) * hd] = n[h] + dx[h][CH:, hd:]

        @pl.when(c < nc - 2)
        def _():
            forward(c + 2)

        @pl.when(c < nc - 1)
        def _():
            far_forward(c + 1)

        @pl.when(c == nc - 2)
        def _():
            for t in range(1, TP):
                to_column(t).start()

        @pl.when(c < nc - 2)
        def _():
            sides(c + 2)

        return carry

    lax.fori_loop(0, nc, chunk, 0)

    def root(h):
        return 4 * core + 2 * h

    def to_root(h):
        return pltpu.make_async_remote_copy(
            src_ref=xbf.at[h], dst_ref=mbuf.at[z], send_sem=msend.at[h], recv_sem=mrecv.at[z],
            device_id={"ctx": base + root(h)}, device_id_type=MESH,
        )

    for h in hs:
        xbf[h] = pref[h].astype(BF16)

        @pl.when(z != root(h))
        def _():
            to_root(h).start()

        @pl.when(z == root(h))
        def _():
            mbuf[z] = xbf[h]

    def to_group(d):
        return pltpu.make_async_remote_copy(
            src_ref=tbuf.at[x], dst_ref=tbuf.at[x], send_sem=tsend.at[d - 1], recv_sem=trecv.at[x],
            device_id={"ctx": lax.rem(ctx + d * Z, X * Z)}, device_id_type=MESH,
        )

    def to_member(h, j):
        return pltpu.make_async_remote_copy(
            src_ref=wob.at[j], dst_ref=win.at[h], send_sem=osend.at[j], recv_sem=orecv.at[h],
            device_id={"ctx": base + j}, device_id_type=MESH,
        )

    is_root = (z == root(0)) | (z == root(1))
    mine = lax.rem(z, 4) // 2

    @pl.when(is_root)
    def _():
        for j in range(Z):
            @pl.when(z != j)
            def _():
                pltpu.make_async_remote_copy(
                    src_ref=mbuf.at[j], dst_ref=mbuf.at[j], send_sem=msend.at[0], recv_sem=mrecv.at[j],
                    device_id={"ctx": base + lax.rem(z + 1, Z)}, device_id_type=MESH,
                ).wait_recv()
        ms = [mbuf[j].astype(F32) for j in range(Z)]
        pr = [compose(ms[2 * j + 1], ms[2 * j], hd) for j in range(Z // 2)]
        qd = [compose(pr[2 * j + 1], pr[2 * j], hd) for j in range(Z // 4)]
        tbuf[x] = compose(qd[1], qd[0], hd).astype(BF16)
        for d in range(1, X):
            @pl.when(x + d < X)
            def _():
                to_group(d).start()
        six = compose(pr[2], qd[0], hd)
        pre = [None, ms[0], pr[0], compose(ms[2], pr[0], hd), qd[0], compose(ms[4], qd[0], hd), six,
               compose(ms[6], six, hd)]
        wst[...] = w0[mine]
        for j in range(X - 1):
            @pl.when(j < x)
            def _():
                pltpu.make_async_remote_copy(
                    src_ref=tbuf.at[j], dst_ref=tbuf.at[j], send_sem=tsend.at[0], recv_sem=trecv.at[j],
                    device_id={"ctx": lax.rem(ctx + Z, X * Z)}, device_id_type=MESH,
                ).wait_recv()
                wst[...] = apply_map(tbuf[j].astype(F32), wst[...], hd)
        w = wst[...]
        for j in range(Z):
            wob[j] = (w if j == 0 else apply_map(pre[j], w, hd)).astype(BF16)
        for j in range(Z):
            @pl.when(z != j)
            def _():
                to_member(mine, j).start()
        win[mine] = wob[z]

    gbegin, gshare, gforward, gfar_forward, garrived, gsent = pair_gather(
        None, ng, width, rows // 2, me, hsend, hrecv)
    for h in hs:
        @pl.when(z != root(h))
        def _():
            pltpu.make_async_remote_copy(
                src_ref=win.at[h], dst_ref=win.at[h], send_sem=osend.at[0], recv_sem=orecv.at[h],
                device_id={"ctx": base + lax.rem(z + 1, Z)}, device_id_type=MESH,
            ).wait_recv()
    for c in range(2):
        rs = slice(c * (rows // 2), (c + 1) * (rows // 2))
        for h in hs:
            hc = slice(h * hd, (h + 1) * hd)
            zv = dot(pbuf[rs, hc], win[h]) + nbuf[rs, hc]
            zv = zv * lax.rsqrt(jnp.mean(zv * zv, -1, keepdims=True) + 1e-06) * gain[h:h + 1, :]
            ng[rs, pl.ds(pl.multiple_of(me * width + h * hd, hd), hd)] = zv.astype(BF16)
        gbegin(c)
        gshare(c)
    for c in range(2):
        gforward(c)
    for t in range(1, TP):
        from_column(t).wait_recv()
    wown.wait()
    for c in range(2):
        gfar_forward(c)
    for c in range(2):
        for kind in (2, 5, 6, 7, 8):
            garrived(kind, c)
        rs = slice(c * (rows // 2), (c + 1) * (rows // 2))
        mixed[rs, :] = jnp.dot(ng[rs, :], wc[...], preferred_element_type=F32).astype(BF16)

    def drain(c, carry):
        sent(c)
        return carry

    lax.fori_loop(0, nc, drain, 0)
    for c in range(2):
        gsent(c)
    for t in range(1, TP):
        to_column(t).wait_send()
    for h in hs:
        @pl.when(z != root(h))
        def _():
            to_root(h).wait_send()

    @pl.when(is_root)
    def _():
        for d in range(1, X):
            @pl.when(x + d < X)
            def _():
                to_group(d).wait_send()
        for j in range(Z):
            @pl.when(z != j)
            def _():
                to_member(mine, j).wait_send()


def vmem_spec():
    return pl.BlockSpec(memory_space=pltpu.VMEM)


def local(hidden_in, w_qkv, lr_weight, inner_lr, init_state, norm_gain, w_out):
    rows, feat = hidden_in.shape
    _, depth, width = w_qkv.shape
    heads, hd = norm_gain.shape
    nc = rows // CH
    out_cols = w_out.shape[1] // TP
    dma = pltpu.SemaphoreType.DMA
    operands = (hidden_in, w_qkv, lr_weight.T, inner_lr, init_state, norm_gain, w_out)
    operands = [pltpu.with_memory_space_constraint(a, pltpu.HBM) for a in operands]
    return pl.pallas_call(
        layer_kernel,
        out_shape=jax.ShapeDtypeStruct((rows, out_cols), BF16),
        in_specs=[pl.BlockSpec(memory_space=pltpu.HBM)] * 7,
        out_specs=vmem_spec(),
        scratch_shapes=[
            pltpu.VMEM((heads, depth), BF16),
            pltpu.SMEM((heads,), F32),
            pltpu.VMEM((heads, hd, hd), F32),
            pltpu.VMEM((heads, hd), F32),
            pltpu.VMEM((rows, depth), BF16),
            pltpu.VMEM((depth, 3 * width + CH), BF16),
            pltpu.VMEM((CH, depth), F32),
            pltpu.VMEM((rows, 3 * width + CH), F32),
            pltpu.VMEM((heads, hd, 2 * hd), F32),
            pltpu.VMEM((rows, width), BF16),
            pltpu.VMEM((rows, width), F32),
            pltpu.VMEM((heads, hd, 2 * hd), BF16),
            pltpu.VMEM((Z, hd, 2 * hd), BF16),
            pltpu.VMEM((X, hd, 2 * hd), BF16),
            pltpu.VMEM((hd, hd), F32),
            pltpu.VMEM((Z, hd, hd), BF16),
            pltpu.VMEM((heads, hd, hd), BF16),
            pltpu.VMEM((rows, TP * width), BF16),
            pltpu.VMEM((TP * width, out_cols), BF16),
            dma((2,)),
            dma((4,)),
            dma((3,)),
            dma((nc, 9)),
            dma((nc, 9)),
            dma((TP - 1,)),
            dma((TP - 1,)),
            dma((heads,)),
            dma((Z,)),
            dma((X - 1,)),
            dma((X,)),
            dma((Z,)),
            dma((heads,)),
            dma((2, 9)),
            dma((2, 9)),
        ],
        compiler_params=pltpu.CompilerParams(
            collective_id=0, has_side_effects=True, vmem_limit_bytes=48 * 1024 * 1024
        ),
        name="layer",
    )(*operands)


def solution(mesh):
    in_specs = (
        P("ctx", "tp"),
        P(None, None, "tp"),
        P(None, "tp"),
        P("tp"),
        P("tp", None, None),
        P("tp", None),
        P("tp", None),
    )
    out_specs = P("ctx", "tp")
    return jax.shard_map(local, mesh=mesh, in_specs=in_specs, out_specs=out_specs, check_vma=False)
```

```python
import jax
import jax.numpy as jnp
from jax import lax
from jax.experimental import pallas as pl
from jax.experimental.pallas import tpu as pltpu
from jax.sharding import PartitionSpec as P

MB = 16
CH = 128
MESH = pl.DeviceIdType.MESH
F32 = jnp.float32
BF16 = jnp.bfloat16
Y, CORES = 4, 2
X, Z = 4, 8
TP = Y * CORES


def dot(a, b):
    return jnp.dot(a.astype(BF16), b.astype(BF16), preferred_element_type=F32)


def compose(later, earlier, hd):
    return earlier + dot(later[:, :hd], earlier) + later


def apply_map(m, w, hd):
    return w + dot(m[:, :hd], w) + m[:, hd:]


def pair_gather(src, buf, span, me, send, recv):
    half = span // 2
    sib = me + 1 - 2 * lax.rem(me, 2)
    up, down, far = lax.rem(me + 2, TP), lax.rem(me + TP - 2, TP), lax.rem(me + 4, TP)
    sup, sdown, sfar = lax.rem(sib + 2, TP), lax.rem(sib + TP - 2, TP), lax.rem(sib + 4, TP)
    target = (up, down, sib, up, down, sib, sib, sib, sib)
    leaving = (me, me, me, down, up, down, up, far, far)
    landing = (down, up, sib, far, far, sdown, sup, sfar, sfar)

    def place(ref, kind, c, owner):
        r0 = half if kind in (4, 8) else 0
        n = half if kind in (3, 4, 7, 8) else span
        rs = pl.ds(pl.multiple_of(c * span + r0, 16), n)
        return ref.at[rs] if owner is None else ref.at[owner, rs]

    def out(kind, c):
        own = src is not None and kind < 3
        return pltpu.make_async_remote_copy(
            src_ref=place(src, kind, c, None) if own else place(buf, kind, c, leaving[kind]),
            dst_ref=place(buf, kind, c, leaving[kind]),
            send_sem=send.at[c, kind],
            recv_sem=recv.at[c, kind],
            device_id={"tp": target[kind]},
            device_id_type=MESH,
        )

    def arrived(kind, c):
        ref = place(buf, kind, c, landing[kind])
        pltpu.make_async_remote_copy(
            src_ref=ref, dst_ref=ref, send_sem=send.at[c, kind], recv_sem=recv.at[c, kind],
            device_id={"tp": sib}, device_id_type=MESH,
        ).wait_recv()

    def begin(c):
        out(0, c).start()
        out(1, c).start()

    def share(c):
        out(2, c).start()

    def forward(c):
        arrived(0, c)
        out(3, c).start()
        out(5, c).start()
        arrived(1, c)
        out(4, c).start()
        out(6, c).start()

    def far_forward(c):
        arrived(3, c)
        out(7, c).start()
        arrived(4, c)
        out(8, c).start()

    def sent(c):
        for kind in range(9):
            out(kind, c).wait_send()

    return begin, share, forward, far_forward, arrived, sent


def layer_kernel(hid, wq, lrw_in, lr_in, w0_in, gain_in, wout, mixed,
                 lrw, lr, w0, gain, gall, xg, wbuf, wgate, lrt, acc, pref, xbf, mbuf, tbuf, pre, wst, wob, pn, wg, abuf, bbuf, total,
                 loc, lsem, wsem, gsend, grecv, psend, precv, hsend, hrecv, msend, mrecv, tsend, trecv, osend, orecv,
                 ysend, yrecv, axsend, axrecv, azsend, azrecv, bzsend, bzrecv, bxsend, bxrecv):
    rows, feat = hid.shape
    nc = rows // CH
    heads, hd = pref.shape[0], pref.shape[1]
    hs = range(heads)
    width = heads * hd
    ocols = mixed.shape[1]
    me = lax.axis_index("tp")
    ctx = lax.axis_index("ctx")
    core = lax.rem(me, 2)
    chip = me // 2
    z = lax.rem(ctx, Z)
    x = ctx // Z
    base = x * Z

    smalls = [
        pltpu.make_async_copy(a, b, lsem.at[i])
        for i, (a, b) in enumerate(((lrw_in, lrw), (lr_in, lr), (w0_in, w0), (gain_in, gain)))
    ]
    for cp in smalls:
        cp.start()
    barrier = pltpu.get_barrier_semaphore()
    for t in range(1, TP):
        pl.semaphore_signal(barrier, inc=1, device_id={"tp": lax.rem(me + t, TP)}, device_id_type=MESH)
    for t in range(1, Z):
        pl.semaphore_signal(barrier, inc=1, device_id={"ctx": base + lax.rem(z + t, Z)}, device_id_type=MESH)
    for t in range(1, X):
        pl.semaphore_signal(barrier, inc=1, device_id={"ctx": lax.rem(ctx + t * Z, X * Z)}, device_id_type=MESH)

    wcopies = [pltpu.make_async_copy(wq.at[c], wbuf.at[c], wsem.at[c]) for c in range(3)]
    for cp in wcopies:
        cp.start()
    own = pltpu.make_async_copy(hid, xg.at[me], loc.at[0])
    own.start()

    bblock = 8 + 2 * x + z // 4
    blocks = ((z, x), (bblock, lax.rem(z, 4)))

    def piece_in(kind, j):
        block, cb = blocks[kind]
        at = pl.multiple_of(j * ocols + cb * CH, CH)
        return wout.at[pl.ds(pl.multiple_of(block * MB, MB), MB), pl.ds(at, CH)]

    def piece(kind, j):
        return abuf.at[z, x, j] if kind == 0 else bbuf.at[x, z, j]

    def pieces(kind, cx, cz):
        return abuf.at[cz, cx] if kind == 0 else bbuf.at[cx, cz]

    def remote(src, dst, ss, rr, to):
        return pltpu.make_async_remote_copy(
            src_ref=src, dst_ref=dst, send_sem=ss, recv_sem=rr, device_id=to, device_id_type=MESH)

    def landed(ref, rr):
        remote(ref, ref, loc.at[0], rr, {"tp": lax.rem(me + 1, TP)}).wait_recv()

    def on_tp(t):
        return {"tp": lax.rem(me + t, TP)}

    def on_z(t):
        return {"ctx": base + lax.rem(z + t, Z)}

    def on_x(t):
        return {"ctx": lax.rem(ctx + t * Z, X * Z)}

    def y_copy(kind, t):
        return remote(piece_in(kind, lax.rem(me + t, TP)), piece(kind, me), ysend.at[kind, t - 1],
                      yrecv.at[kind, t - 1], on_tp(t))

    def gain_copy(t):
        return remote(gall.at[me], gall.at[me], ysend.at[2, t - 1], yrecv.at[2, t - 1], on_tp(t))

    def ax_copy(t):
        ref = pieces(0, x, z)
        return remote(ref, ref, axsend.at[t - 1], axrecv.at[t - 1], on_x(t))

    def bz_copy(t):
        ref = pieces(1, x, z)
        return remote(ref, ref, bzsend.at[t - 1], bzrecv.at[t - 1], on_z(t))

    def b_rows(cx):
        return bbuf.at[cx]

    def bx_copy(t):
        return remote(b_rows(x), b_rows(x), bxsend.at[t - 1], bxrecv.at[t - 1], on_x(t))

    az_hops = (1, 2, Z - 1, Z - 2, 1, Z - 1, 2, Z - 2)
    az_from = (0, 0, 0, 0, Z - 2, 2, Z - 2, 2)

    def az_ref(k, block):
        block = lax.rem(block + 2 * Z, Z)
        if k < 6:
            return abuf.at[block]
        return abuf.at[block, pl.ds((k - 6) * (X // 2), X // 2)]

    def az_copy(k):
        ref = az_ref(k, z + az_from[k])
        return remote(ref, ref, azsend.at[k], azrecv.at[k], on_z(az_hops[k]))

    def az_landed(k):
        landed(az_ref(k, z + az_from[k] - az_hops[k]), azrecv.at[k])

    def az_near():
        for k in (1, 3, 0, 2):
            az_copy(k).start()

    def az_far():
        az_landed(1)
        az_landed(3)
        for k in range(4, 8):
            az_copy(k).start()

    def spread_first():
        for t in range(1, TP):
            j = lax.rem(me + TP - t, TP)
            landed(piece(0, j), yrecv.at[0, t - 1])
            landed(piece(1, j), yrecv.at[1, t - 1])
        for cp in wown:
            cp.wait()
        for t in range(1, X):
            ax_copy(t).start()
        for t in range(1, Z):
            bz_copy(t).start()

    def spread_z():
        for t in range(1, X):
            landed(pieces(0, lax.rem(x + X - t, X), z), axrecv.at[t - 1])
        az_near()

    def spread_x():
        for t in range(1, Z):
            landed(pieces(1, x, lax.rem(z + Z - t, Z)), bzrecv.at[t - 1])
        for t in range(1, X):
            bx_copy(t).start()

    wown = [pltpu.make_async_copy(piece_in(kind, me), piece(kind, me), loc.at[1 + kind]) for kind in range(2)]
    for cp in wown:
        cp.start()
    begin, share, forward, far_forward, arrived, sent = pair_gather(hid, xg, CH, me, gsend, grecv)
    pbegin, pshare, pforward, pfar_forward, parrived, psent = pair_gather(None, pn, CH, me, psend, precv)
    pl.semaphore_wait(barrier, TP + Z + X - 3)
    begin(0)
    begin(1)
    for c in range(nc):
        share(c)
    for t in range(1, TP):
        y_copy(0, t).start()
        y_copy(1, t).start()

    lrt[...] = jnp.zeros_like(lrt)
    for cp in smalls:
        cp.wait()
    gall[me] = jnp.zeros_like(gall[me])
    gall[me, 0:heads, :] = gain[...]
    for t in range(1, TP):
        gain_copy(t).start()
    lrt[0:heads, :] = lrw[...].astype(F32)

    def gate(i, carry):
        at = pl.ds(pl.multiple_of(i * CH, CH), CH)
        wgate[at, :] = lrt[:, at].T.astype(BF16)
        return carry

    lax.fori_loop(0, wgate.shape[0] // CH, gate, 0)
    pref[...] = jnp.zeros_like(pref)
    own.wait()
    for cp in wcopies:
        cp.wait()

    def part(c, q):
        rs = pl.ds(pl.multiple_of(c * CH, CH), CH)
        cj = lax.rem(chip + q, Y)
        ks = pl.ds(pl.multiple_of(cj * 2 * feat, 2 * feat), 2 * feat)
        xs = jnp.concatenate([xg[2 * cj, rs], xg[2 * cj + 1, rs]], 1)
        weights = [wbuf[i, ks, :] for i in range(3)] + [wgate[ks, :]]
        return jnp.concatenate([jnp.dot(xs, w, preferred_element_type=F32) for w in weights], 1)

    def near(c, carry):
        arrived(2, c)
        acc[pl.ds(pl.multiple_of(c * CH, CH), CH), :] = part(c, 0)
        return carry

    def sides(c):
        arrived(5, c)
        arrived(6, c)
        acc[pl.ds(pl.multiple_of(c * CH, CH), CH), :] += part(c, 1) + part(c, Y - 1)

    lax.fori_loop(0, nc, near, 0)
    forward(0)
    begin(2)
    spread_first()
    sides(0)
    forward(1)
    begin(3)
    far_forward(0)
    sides(1)

    row = lax.broadcasted_iota(jnp.int32, (CH, CH), 0)
    col = lax.broadcasted_iota(jnp.int32, (CH, CH), 1)
    causal = row >= col
    before = (row >> 4) > (col >> 4)

    def chunk(c, carry):
        arrived(7, c)
        arrived(8, c)
        rs = pl.ds(pl.multiple_of(c * CH, CH), CH)
        proj = acc[rs, :] + part(c, 2)
        part3 = [[proj[:, (k * heads + h) * hd:(k * heads + h + 1) * hd] for h in hs] for k in range(3)]

        def unit(v):
            return v * lax.rsqrt(jnp.sum(v * v, -1, keepdims=True) + hd * 1e-06)

        q = [unit(part3[0][h]) for h in hs]
        k = [unit(part3[1][h]) for h in hs]
        rate = [lr[h] * jax.nn.sigmoid(proj[:, 3 * width + h:3 * width + h + 1]) for h in hs]
        krt = [(k[h] * rate[h]).T.astype(BF16) for h in hs]
        sg = [dot(jnp.concatenate([q[h], k[h]], 0), krt[h]) for h in hs]
        m = [jnp.where(causal, sg[h][:CH], 0.0).astype(BF16) for h in hs]
        l1 = [jnp.where(before, sg[h][CH:], 0.0) for h in hs]
        lb = [l1[h].astype(BF16) for h in hs]
        l2 = [dot(lb[h], lb[h]) for h in hs]
        l34 = [dot(jnp.concatenate([lb[h], l2[h].astype(BF16)], 0), l2[h]) for h in hs]
        t1 = [l2[h] - l1[h] - l34[h][:CH] for h in hs]
        t = [t1[h] + l34[h][CH:] + dot(t1[h], l34[h][CH:]) for h in hs]
        kv = [jnp.concatenate([k[h], part3[2][h]], 1) for h in hs]
        uy = [kv[h] + dot(t[h], kv[h]) for h in hs]
        dn = [dot(jnp.concatenate([krt[h], m[h]], 0), uy[h]) for h in hs]
        d = [jnp.concatenate([-dn[h][:CH, :hd], dn[h][:CH, hd:]], 1) for h in hs]
        p = [q[h] - dn[h][CH:, :hd] for h in hs]
        n = [dn[h][CH:, hd:] for h in hs]
        x0 = [pref[h] for h in hs]
        dx = [dot(jnp.concatenate([d[h][:, :hd], p[h]], 0), x0[h]) for h in hs]
        for h in hs:
            pref[h] = x0[h] + dx[h][:CH] + d[h]
            pn[me, rs, h * hd:(h + 1) * hd] = (p[h] + dx[h][CH:, :hd]).astype(BF16)
            pn[me, rs, width + h * hd:width + (h + 1) * hd] = (n[h] + dx[h][CH:, hd:]).astype(BF16)

        @pl.when(c < nc - 2)
        def _():
            forward(c + 2)

        @pl.when(c < nc - 1)
        def _():
            far_forward(c + 1)

        @pl.when(c == nc - 2)
        def _():
            for k in range(nc - 1):
                pbegin(k)
                pshare(k)

        @pl.when(c < nc - 2)
        def _():
            sides(c + 2)

        @pl.when(c == 0)
        def _():
            spread_z()

        @pl.when(c == 1)
        def _():
            spread_x()

        return carry

    lax.fori_loop(0, nc, chunk, 0)

    def root(h):
        return 4 * core + 2 * h

    def to_root(h):
        return pltpu.make_async_remote_copy(
            src_ref=xbf.at[h], dst_ref=mbuf.at[z], send_sem=msend.at[h], recv_sem=mrecv.at[z],
            device_id={"ctx": base + root(h)}, device_id_type=MESH,
        )

    for h in hs:
        xbf[h] = pref[h].astype(BF16)

        @pl.when(z != root(h))
        def _():
            to_root(h).start()

        @pl.when(z == root(h))
        def _():
            mbuf[z] = xbf[h]

    pbegin(nc - 1)
    pshare(nc - 1)
    pforward(0)
    az_far()
    pforward(1)

    def to_group(d):
        return remote(tbuf.at[x], tbuf.at[x], tsend.at[d - 1], trecv.at[x], on_x(d))

    def state_at(h):
        return wg.at[me, pl.ds(pl.multiple_of(h * hd, hd), hd)]

    def to_member(h, j):
        return remote(wob.at[j], state_at(h), osend.at[j], orecv.at[h], {"ctx": base + j})

    is_root = (z == root(0)) | (z == root(1))
    mine = lax.rem(z, 4) // 2

    @pl.when(is_root)
    def _():
        for j in range(Z):
            @pl.when(z != j)
            def _():
                landed(mbuf.at[j], mrecv.at[j])
        ms = [mbuf[j].astype(F32) for j in range(Z)]
        pr = [compose(ms[2 * j + 1], ms[2 * j], hd) for j in range(Z // 2)]
        qd = [compose(pr[2 * j + 1], pr[2 * j], hd) for j in range(Z // 4)]
        tbuf[x] = compose(qd[1], qd[0], hd).astype(BF16)
        for d in range(1, X):
            @pl.when(x + d < X)
            def _():
                to_group(d).start()
        six = compose(pr[2], qd[0], hd)
        for j, m in enumerate((ms[0], pr[0], compose(ms[2], pr[0], hd), qd[0], compose(ms[4], qd[0], hd), six,
                               compose(ms[6], six, hd))):
            pre[j] = m

    pforward(2)
    pfar_forward(0)

    @pl.when(is_root)
    def _():
        wst[...] = w0[mine]
        for j in range(X - 1):
            @pl.when(j < x)
            def _():
                landed(tbuf.at[j], trecv.at[j])
                wst[...] = apply_map(tbuf[j].astype(F32), wst[...], hd)
        w = wst[...]
        wob[0] = w.astype(BF16)
        for j in range(1, Z):
            wob[j] = apply_map(pre[j - 1], w, hd).astype(BF16)
        for j in range(Z):
            @pl.when(z != j)
            def _():
                to_member(mine, j).start()
        wg[me, pl.ds(pl.multiple_of(mine * hd, hd), hd)] = wob[z]

    pforward(3)
    for c in range(1, nc):
        pfar_forward(c)
    for h in hs:
        @pl.when(z != root(h))
        def _():
            landed(state_at(h), orecv.at[h])
    far = {"tp": lax.rem(me + 4, TP)}
    sib = me + 1 - 2 * core
    hop = ({"tp": lax.rem(me + 2, TP)}, {"tp": lax.rem(me + TP - 2, TP)}, far) + ({"tp": sib},) * 4
    from_me = (0, 0, 0, 0, TP - 2, 2, 4)
    to_me = (me + TP - 2, me + 2, me + 4, sib, sib + TP - 2, sib + 2, sib + 4)

    def states(j):
        return wg.at[lax.rem(j, TP)]

    def state_copy(kind):
        ref = states(me + from_me[kind])
        return remote(ref, ref, hsend.at[kind], hrecv.at[kind], hop[kind])

    def state_landed(kind):
        landed(states(to_me[kind]), hrecv.at[kind])

    for kind in range(4):
        state_copy(kind).start()
    for k in (0, 2, 4, 5, 6, 7):
        az_landed(k)
    for t in range(1, X):
        landed(b_rows(lax.rem(x + X - t, X)), bxrecv.at[t - 1])
    for t in range(1, TP):
        landed(gall.at[lax.rem(me + TP - t, TP)], yrecv.at[2, t - 1])

    def heads_of(q, first, last):
        cj = lax.rem(chip + q, Y)
        blocks_w, parts = [], []
        for k in range(2):
            j = 2 * cj + k
            top = [abuf[:, cx, j].reshape(CH, CH) for cx in range(X)]
            low = [jnp.concatenate([bbuf[cx, zr * 4 + cz, j] for cx in range(X) for zr in range(2)], 0)
                   for cz in range(4)]
            blocks_w += [jnp.concatenate(top, 1), jnp.concatenate(low, 1)]
            for h in hs:
                hc = slice(h * hd, (h + 1) * hd)
                zv = dot(pn[j, :, hc], wg[j, hc, :]) + pn[j, :, width + h * hd:width + (h + 1) * hd].astype(F32)
                zv = zv * lax.rsqrt(jnp.mean(zv * zv, -1, keepdims=True) + 1e-06)
                parts.append((zv * gall[j, h:h + 1, :]).astype(BF16))
        term = jnp.dot(jnp.concatenate(parts, 1), jnp.concatenate(blocks_w, 0), preferred_element_type=F32)
        if not first:
            term = total[:, :] + term
        if last:
            mixed[:, :] = term.astype(BF16)
        else:
            total[:, :] = term

    def gathered(*kinds):
        for kind in kinds:
            for c in range(nc):
                parrived(kind, c)

    gathered(2)
    state_landed(3)
    heads_of(0, True, False)
    for kind in range(3):
        state_landed(kind)
        state_copy(kind + 4).start()
    gathered(5, 6)
    state_landed(4)
    heads_of(Y - 1, False, False)
    state_landed(5)
    heads_of(1, False, False)
    gathered(7, 8)
    state_landed(6)
    heads_of(2, False, True)

    def drain(c, carry):
        sent(c)
        psent(c)
        return carry

    lax.fori_loop(0, nc, drain, 0)
    for kind in range(7):
        state_copy(kind).wait_send()
    for t in range(1, TP):
        y_copy(0, t).wait_send()
        y_copy(1, t).wait_send()
        gain_copy(t).wait_send()
    for t in range(1, X):
        ax_copy(t).wait_send()
        bx_copy(t).wait_send()
    for t in range(1, Z):
        bz_copy(t).wait_send()
    for k in range(8):
        az_copy(k).wait_send()
    for h in hs:
        @pl.when(z != root(h))
        def _():
            to_root(h).wait_send()

    @pl.when(is_root)
    def _():
        for d in range(1, X):
            @pl.when(x + d < X)
            def _():
                to_group(d).wait_send()
        for j in range(Z):
            @pl.when(z != j)
            def _():
                to_member(mine, j).wait_send()


def vmem_spec():
    return pl.BlockSpec(memory_space=pltpu.VMEM)


def local(hidden_in, w_qkv, lr_weight, inner_lr, init_state, norm_gain, w_out):
    rows, feat = hidden_in.shape
    _, depth, width = w_qkv.shape
    heads, hd = norm_gain.shape
    nc = rows // CH
    out_cols = w_out.shape[1] // TP
    dma = pltpu.SemaphoreType.DMA
    operands = (hidden_in, w_qkv, lr_weight.T, inner_lr, init_state, norm_gain, w_out)
    operands = [pltpu.with_memory_space_constraint(a, pltpu.HBM) for a in operands]
    return pl.pallas_call(
        layer_kernel,
        out_shape=jax.ShapeDtypeStruct((rows, out_cols), BF16),
        in_specs=[pl.BlockSpec(memory_space=pltpu.HBM)] * 7,
        out_specs=vmem_spec(),
        scratch_shapes=[
            pltpu.VMEM((heads, depth), BF16),
            pltpu.SMEM((heads,), F32),
            pltpu.VMEM((heads, hd, hd), F32),
            pltpu.VMEM((heads, hd), F32),
            pltpu.VMEM((TP, 8, hd), F32),
            pltpu.VMEM((TP, rows, feat), BF16),
            pltpu.VMEM((3, depth, width), BF16),
            pltpu.VMEM((depth, CH), BF16),
            pltpu.VMEM((CH, depth), F32),
            pltpu.VMEM((rows, 3 * width + CH), F32),
            pltpu.VMEM((heads, hd, 2 * hd), F32),
            pltpu.VMEM((heads, hd, 2 * hd), BF16),
            pltpu.VMEM((Z, hd, 2 * hd), BF16),
            pltpu.VMEM((X, hd, 2 * hd), BF16),
            pltpu.VMEM((Z - 1, hd, 2 * hd), F32),
            pltpu.VMEM((hd, hd), F32),
            pltpu.VMEM((Z, hd, hd), BF16),
            pltpu.VMEM((TP, rows, 2 * width), BF16),
            pltpu.VMEM((TP, width, hd), BF16),
            pltpu.VMEM((Z, X, TP, MB, CH), BF16),
            pltpu.VMEM((X, Z, TP, MB, CH), BF16),
            pltpu.VMEM((rows, out_cols), F32),
            dma((3,)),
            dma((4,)),
            dma((3,)),
            dma((nc, 9)),
            dma((nc, 9)),
            dma((nc, 9)),
            dma((nc, 9)),
            dma((7,)),
            dma((7,)),
            dma((heads,)),
            dma((Z,)),
            dma((X - 1,)),
            dma((X,)),
            dma((Z,)),
            dma((heads,)),
            dma((3, TP - 1)),
            dma((3, TP - 1)),
            dma((X - 1,)),
            dma((X - 1,)),
            dma((8,)),
            dma((8,)),
            dma((Z - 1,)),
            dma((Z - 1,)),
            dma((X - 1,)),
            dma((X - 1,)),
        ],
        compiler_params=pltpu.CompilerParams(
            collective_id=0, has_side_effects=True, vmem_limit_bytes=48 * 1024 * 1024
        ),
        name="layer",
    )(*operands)


def solution(mesh):
    in_specs = (
        P("ctx", "tp"),
        P(None, None, "tp"),
        P(None, "tp"),
        P("tp"),
        P("tp", None, None),
        P("tp", None),
        P("tp", None),
    )
    out_specs = P("ctx", "tp")
    return jax.shard_map(local, mesh=mesh, in_specs=in_specs, out_specs=out_specs, check_vma=False)
```

```python
import jax
import jax.numpy as jnp
from jax import lax
from jax.experimental import pallas as pl
from jax.experimental.pallas import tpu as pltpu
from jax.sharding import PartitionSpec as P

MB = 16
CH = 128
MESH = pl.DeviceIdType.MESH
F32 = jnp.float32
BF16 = jnp.bfloat16
Y, CORES = 4, 2
X, Z = 4, 8
TP = Y * CORES


def dot(a, b):
    return jnp.dot(a.astype(BF16), b.astype(BF16), preferred_element_type=F32)


def compose(later, earlier, hd):
    return earlier + dot(later[:, :hd], earlier) + later


def apply_map(m, w, hd):
    return w + dot(m[:, :hd], w) + m[:, hd:]


def pair_gather(src, buf, span, me, send, recv):
    half = span // 2
    sib = me + 1 - 2 * lax.rem(me, 2)
    up, down, far = lax.rem(me + 2, TP), lax.rem(me + TP - 2, TP), lax.rem(me + 4, TP)
    sup, sdown, sfar = lax.rem(sib + 2, TP), lax.rem(sib + TP - 2, TP), lax.rem(sib + 4, TP)
    target = (up, down, sib, up, down, sib, sib, sib, sib)
    leaving = (me, me, me, down, up, down, up, far, far)
    landing = (down, up, sib, far, far, sdown, sup, sfar, sfar)

    def place(ref, kind, c, owner):
        r0 = half if kind in (4, 8) else 0
        n = half if kind in (3, 4, 7, 8) else span
        rs = pl.ds(pl.multiple_of(c * span + r0, 16), n)
        return ref.at[rs] if owner is None else ref.at[owner, rs]

    def out(kind, c):
        own = src is not None and kind < 3
        return pltpu.make_async_remote_copy(
            src_ref=place(src, kind, c, None) if own else place(buf, kind, c, leaving[kind]),
            dst_ref=place(buf, kind, c, leaving[kind]),
            send_sem=send.at[c, kind],
            recv_sem=recv.at[c, kind],
            device_id={"tp": target[kind]},
            device_id_type=MESH,
        )

    def arrived(kind, c):
        ref = place(buf, kind, c, landing[kind])
        pltpu.make_async_remote_copy(
            src_ref=ref, dst_ref=ref, send_sem=send.at[c, kind], recv_sem=recv.at[c, kind],
            device_id={"tp": sib}, device_id_type=MESH,
        ).wait_recv()

    def begin(c):
        out(0, c).start()
        out(1, c).start()

    def share(c):
        out(2, c).start()

    def forward(c):
        arrived(0, c)
        out(3, c).start()
        out(5, c).start()
        arrived(1, c)
        out(4, c).start()
        out(6, c).start()

    def far_forward(c):
        arrived(3, c)
        out(7, c).start()
        arrived(4, c)
        out(8, c).start()

    def sent(c):
        for kind in range(9):
            out(kind, c).wait_send()

    return begin, share, forward, far_forward, arrived, sent


def layer_kernel(hid, wq, lrw_in, lr_in, w0_in, gain_in, wout, mixed,
                 lrw, lr, w0, gain, gall, xg, wbuf, wgate, lrt, acc, pref, xbf, mbuf, tbuf, pre, wst, wob, pn, wg, abuf, bbuf, total,
                 loc, lsem, wsem, gsend, grecv, psend, precv, hsend, hrecv, msend, mrecv, tsend, trecv, osend, orecv,
                 ysend, yrecv, axsend, axrecv, azsend, azrecv, bzsend, bzrecv, bxsend, bxrecv):
    rows, feat = hid.shape
    nc = rows // CH
    heads, hd = pref.shape[0], pref.shape[1]
    hs = range(heads)
    width = heads * hd
    ocols = mixed.shape[1]
    me = lax.axis_index("tp")
    ctx = lax.axis_index("ctx")
    core = lax.rem(me, 2)
    chip = me // 2
    z = lax.rem(ctx, Z)
    x = ctx // Z
    base = x * Z

    smalls = [
        pltpu.make_async_copy(a, b, lsem.at[i])
        for i, (a, b) in enumerate(((lrw_in, lrw), (lr_in, lr), (w0_in, w0), (gain_in, gain)))
    ]
    for cp in smalls:
        cp.start()
    barrier = pltpu.get_barrier_semaphore()
    for t in range(1, TP):
        pl.semaphore_signal(barrier, inc=1, device_id={"tp": lax.rem(me + t, TP)}, device_id_type=MESH)
    for t in range(1, Z):
        pl.semaphore_signal(barrier, inc=1, device_id={"ctx": base + lax.rem(z + t, Z)}, device_id_type=MESH)
    for t in range(1, X):
        pl.semaphore_signal(barrier, inc=1, device_id={"ctx": lax.rem(ctx + t * Z, X * Z)}, device_id_type=MESH)

    wcopies = [pltpu.make_async_copy(wq.at[c], wbuf.at[c], wsem.at[c]) for c in range(3)]
    for cp in wcopies:
        cp.start()
    own = pltpu.make_async_copy(hid, xg.at[me], loc.at[0])
    own.start()

    bblock = 8 + 2 * x + z // 4
    blocks = ((z, x), (bblock, lax.rem(z, 4)))

    def piece_in(kind, j):
        block, cb = blocks[kind]
        at = pl.multiple_of(j * ocols + cb * CH, CH)
        return wout.at[pl.ds(pl.multiple_of(block * MB, MB), MB), pl.ds(at, CH)]

    def piece(kind, j):
        return abuf.at[z, x, j] if kind == 0 else bbuf.at[x, z, j]

    def pieces(kind, cx, cz):
        return abuf.at[cz, cx] if kind == 0 else bbuf.at[cx, cz]

    def remote(src, dst, ss, rr, to):
        return pltpu.make_async_remote_copy(
            src_ref=src, dst_ref=dst, send_sem=ss, recv_sem=rr, device_id=to, device_id_type=MESH)

    def landed(ref, rr):
        remote(ref, ref, loc.at[0], rr, {"tp": lax.rem(me + 1, TP)}).wait_recv()

    def on_tp(t):
        return {"tp": lax.rem(me + t, TP)}

    def on_z(t):
        return {"ctx": base + lax.rem(z + t, Z)}

    def on_x(t):
        return {"ctx": lax.rem(ctx + t * Z, X * Z)}

    def y_copy(kind, t):
        return remote(piece_in(kind, lax.rem(me + t, TP)), piece(kind, me), ysend.at[kind, t - 1],
                      yrecv.at[kind, t - 1], on_tp(t))

    def gain_copy(t):
        return remote(gall.at[me], gall.at[me], ysend.at[2, t - 1], yrecv.at[2, t - 1], on_tp(t))

    def ax_copy(t):
        ref = pieces(0, x, z)
        return remote(ref, ref, axsend.at[t - 1], axrecv.at[t - 1], on_x(t))

    def bz_copy(t):
        ref = pieces(1, x, z)
        return remote(ref, ref, bzsend.at[t - 1], bzrecv.at[t - 1], on_z(t))

    def b_rows(cx):
        return bbuf.at[cx]

    def bx_copy(t):
        return remote(b_rows(x), b_rows(x), bxsend.at[t - 1], bxrecv.at[t - 1], on_x(t))

    az_hops = (1, 2, Z - 1, Z - 2, 1, Z - 1, 2, Z - 2)
    az_from = (0, 0, 0, 0, Z - 2, 2, Z - 2, 2)

    def az_ref(k, block):
        block = lax.rem(block + 2 * Z, Z)
        if k < 6:
            return abuf.at[block]
        return abuf.at[block, pl.ds((k - 6) * (X // 2), X // 2)]

    def az_copy(k):
        ref = az_ref(k, z + az_from[k])
        return remote(ref, ref, azsend.at[k], azrecv.at[k], on_z(az_hops[k]))

    def az_landed(k):
        landed(az_ref(k, z + az_from[k] - az_hops[k]), azrecv.at[k])

    def az_near():
        for k in (1, 3, 0, 2):
            az_copy(k).start()

    def az_far():
        az_landed(1)
        az_landed(3)
        for k in range(4, 8):
            az_copy(k).start()

    def spread_first():
        for t in range(1, TP):
            j = lax.rem(me + TP - t, TP)
            landed(piece(0, j), yrecv.at[0, t - 1])
            landed(piece(1, j), yrecv.at[1, t - 1])
        for cp in wown:
            cp.wait()
        for t in range(1, X):
            ax_copy(t).start()
        for t in range(1, Z):
            bz_copy(t).start()

    def spread_z():
        for t in range(1, X):
            landed(pieces(0, lax.rem(x + X - t, X), z), axrecv.at[t - 1])
        az_near()

    def spread_x():
        for t in range(1, Z):
            landed(pieces(1, x, lax.rem(z + Z - t, Z)), bzrecv.at[t - 1])
        for t in range(1, X):
            bx_copy(t).start()

    wown = [pltpu.make_async_copy(piece_in(kind, me), piece(kind, me), loc.at[1 + kind]) for kind in range(2)]
    for cp in wown:
        cp.start()
    begin, share, forward, far_forward, arrived, sent = pair_gather(hid, xg, CH, me, gsend, grecv)
    pbegin, pshare, pforward, pfar_forward, parrived, psent = pair_gather(None, pn, CH, me, psend, precv)
    pl.semaphore_wait(barrier, TP + Z + X - 3)
    begin(0)
    begin(1)
    for c in range(nc):
        share(c)

    lrt[...] = jnp.zeros_like(lrt)
    for cp in smalls:
        cp.wait()
    gall[me] = jnp.zeros_like(gall[me])
    gall[me, 0:heads, :] = gain[...]
    for t in range(1, TP):
        gain_copy(t).start()
    lrt[0:heads, :] = lrw[...].astype(F32)

    def gate(i, carry):
        at = pl.ds(pl.multiple_of(i * CH, CH), CH)
        wgate[at, :] = lrt[:, at].T.astype(BF16)
        return carry

    lax.fori_loop(0, wgate.shape[0] // CH, gate, 0)
    pref[...] = jnp.zeros_like(pref)
    for t in range(1, TP):
        y_copy(0, t).start()
        y_copy(1, t).start()
    own.wait()
    for cp in wcopies:
        cp.wait()

    def part(rs, q):
        cj = lax.rem(chip + q, Y)
        ks = pl.ds(pl.multiple_of(cj * 2 * feat, 2 * feat), 2 * feat)
        xs = jnp.concatenate([xg[2 * cj, rs], xg[2 * cj + 1, rs]], 1)
        weights = [wbuf[i, ks, :] for i in range(3)] + [wgate[ks, :]]
        return jnp.concatenate([jnp.dot(xs, w, preferred_element_type=F32) for w in weights], 1)

    def near():
        for c in range(nc):
            arrived(2, c)
        acc[...] = part(pl.ds(0, rows), 0)

    def sides(c):
        arrived(5, c)
        arrived(6, c)
        rs = pl.ds(pl.multiple_of(c * CH, CH), CH)
        acc[rs, :] += part(rs, 1) + part(rs, Y - 1)

    near()
    forward(0)
    begin(2)
    spread_first()
    sides(0)
    forward(1)
    begin(3)
    far_forward(0)
    sides(1)

    row = lax.broadcasted_iota(jnp.int32, (CH, CH), 0)
    col = lax.broadcasted_iota(jnp.int32, (CH, CH), 1)
    causal = row >= col
    before = (row >> 4) > (col >> 4)

    def chunk(c, carry):
        arrived(7, c)
        arrived(8, c)
        rs = pl.ds(pl.multiple_of(c * CH, CH), CH)
        proj = acc[rs, :] + part(rs, 2)
        part3 = [[proj[:, (k * heads + h) * hd:(k * heads + h + 1) * hd] for h in hs] for k in range(3)]

        def unit(v):
            return v * lax.rsqrt(jnp.sum(v * v, -1, keepdims=True) + hd * 1e-06)

        q = [unit(part3[0][h]) for h in hs]
        k = [unit(part3[1][h]) for h in hs]
        rate = [lr[h] * jax.nn.sigmoid(proj[:, 3 * width + h:3 * width + h + 1]) for h in hs]
        krt = [(k[h] * rate[h]).T.astype(BF16) for h in hs]
        qk = [jnp.concatenate([q[h], k[h]], 0).astype(BF16) for h in hs]
        sg = [dot(qk[h], krt[h]) for h in hs]
        x0 = [pref[h] for h in hs]
        qkx = [dot(qk[h], x0[h]) for h in hs]
        r = [qkx[h][CH:] + jnp.concatenate([k[h], -part3[2][h]], 1) for h in hs]
        m = [jnp.where(causal, sg[h][:CH], 0.0).astype(BF16) for h in hs]
        l1 = [jnp.where(before, sg[h][CH:], 0.0) for h in hs]
        lb = [l1[h].astype(BF16) for h in hs]
        l2 = [dot(lb[h], lb[h]) for h in hs]
        l34 = [dot(jnp.concatenate([lb[h], l2[h].astype(BF16)], 0), l2[h]) for h in hs]
        t1 = [l2[h] - l1[h] - l34[h][:CH] for h in hs]
        t = [t1[h] + l34[h][CH:] + dot(t1[h], l34[h][CH:]) for h in hs]
        e = [r[h] + dot(t[h], r[h]) for h in hs]
        dn = [dot(jnp.concatenate([krt[h], m[h]], 0), e[h]) for h in hs]
        for h in hs:
            pref[h] = x0[h] - dn[h][:CH]
            p = q[h] + qkx[h][:CH, :hd] - dn[h][CH:, :hd]
            n = qkx[h][:CH, hd:] - dn[h][CH:, hd:]
            pn[me, rs, h * hd:(h + 1) * hd] = p.astype(BF16)
            pn[me, rs, width + h * hd:width + (h + 1) * hd] = n.astype(BF16)

        @pl.when(c < nc - 2)
        def _():
            forward(c + 2)

        @pl.when(c < nc - 1)
        def _():
            far_forward(c + 1)

        @pl.when(c == nc - 2)
        def _():
            pbegin(2)
            pshare(2)

        @pl.when(c < nc - 2)
        def _():
            sides(c + 2)

        @pl.when(c == 1)
        def _():
            for k in range(2):
                pbegin(k)
                pshare(k)

        @pl.when(c == 0)
        def _():
            spread_z()

        @pl.when(c == 1)
        def _():
            spread_x()

        return carry

    lax.fori_loop(0, nc, chunk, 0)

    def root(h):
        return 4 * core + 2 * h

    def to_root(h):
        return pltpu.make_async_remote_copy(
            src_ref=xbf.at[h], dst_ref=mbuf.at[z], send_sem=msend.at[h], recv_sem=mrecv.at[z],
            device_id={"ctx": base + root(h)}, device_id_type=MESH,
        )

    for h in hs:
        xbf[h] = pref[h].astype(BF16)

        @pl.when(z != root(h))
        def _():
            to_root(h).start()

        @pl.when(z == root(h))
        def _():
            mbuf[z] = xbf[h]

    pbegin(nc - 1)
    pshare(nc - 1)
    pforward(0)
    pforward(1)

    def to_group(d):
        return remote(tbuf.at[x], tbuf.at[x], tsend.at[d - 1], trecv.at[x], on_x(d))

    def state_at(h):
        return wg.at[me, pl.ds(pl.multiple_of(h * hd, hd), hd)]

    def to_member(h, j):
        return remote(wob.at[j], state_at(h), osend.at[j], orecv.at[h], {"ctx": base + j})

    is_root = (z == root(0)) | (z == root(1))
    mine = lax.rem(z, 4) // 2

    @pl.when(is_root)
    def _():
        for j in range(Z):
            @pl.when(z != j)
            def _():
                landed(mbuf.at[j], mrecv.at[j])
        ms = [mbuf[j].astype(F32) for j in range(Z)]
        pr = [compose(ms[2 * j + 1], ms[2 * j], hd) for j in range(Z // 2)]
        qd = [compose(pr[2 * j + 1], pr[2 * j], hd) for j in range(Z // 4)]
        tbuf[x] = compose(qd[1], qd[0], hd).astype(BF16)
        for d in range(1, X):
            @pl.when(x + d < X)
            def _():
                to_group(d).start()
        six = compose(pr[2], qd[0], hd)
        for j, m in enumerate((ms[0], pr[0], compose(ms[2], pr[0], hd), qd[0], compose(ms[4], qd[0], hd), six,
                               compose(ms[6], six, hd))):
            pre[j] = m

    pforward(2)

    @pl.when(is_root)
    def _():
        wst[...] = w0[mine]
        for j in range(X - 1):
            @pl.when(j < x)
            def _():
                landed(tbuf.at[j], trecv.at[j])
                wst[...] = apply_map(tbuf[j].astype(F32), wst[...], hd)
        w = wst[...]
        wob[0] = w.astype(BF16)
        for j in range(1, Z):
            wob[j] = apply_map(pre[j - 1], w, hd).astype(BF16)
        for j in range(Z):
            @pl.when(z != j)
            def _():
                to_member(mine, j).start()
        wg[me, pl.ds(pl.multiple_of(mine * hd, hd), hd)] = wob[z]

    pforward(3)
    az_far()
    for c in range(nc):
        pfar_forward(c)
    for h in hs:
        @pl.when(z != root(h))
        def _():
            landed(state_at(h), orecv.at[h])
    far = {"tp": lax.rem(me + 4, TP)}
    sib = me + 1 - 2 * core
    hop = ({"tp": lax.rem(me + 2, TP)}, {"tp": lax.rem(me + TP - 2, TP)}, far) + ({"tp": sib},) * 4
    from_me = (0, 0, 0, 0, TP - 2, 2, 4)
    to_me = (me + TP - 2, me + 2, me + 4, sib, sib + TP - 2, sib + 2, sib + 4)

    def states(j):
        return wg.at[lax.rem(j, TP)]

    def state_copy(kind):
        ref = states(me + from_me[kind])
        return remote(ref, ref, hsend.at[kind], hrecv.at[kind], hop[kind])

    def state_landed(kind):
        landed(states(to_me[kind]), hrecv.at[kind])

    for kind in range(4):
        state_copy(kind).start()
    for k in (0, 2, 4, 5, 6, 7):
        az_landed(k)
    for t in range(1, X):
        landed(b_rows(lax.rem(x + X - t, X)), bxrecv.at[t - 1])
    for t in range(1, TP):
        landed(gall.at[lax.rem(me + TP - t, TP)], yrecv.at[2, t - 1])

    def heads_of(q, first, last):
        cj = lax.rem(chip + q, Y)
        blocks_w, parts = [], []
        for k in range(2):
            j = 2 * cj + k
            top = [abuf[:, cx, j].reshape(CH, CH) for cx in range(X)]
            low = [jnp.concatenate([bbuf[cx, zr * 4 + cz, j] for cx in range(X) for zr in range(2)], 0)
                   for cz in range(4)]
            blocks_w += [jnp.concatenate(top, 1), jnp.concatenate(low, 1)]
            for h in hs:
                hc = slice(h * hd, (h + 1) * hd)
                zv = dot(pn[j, :, hc], wg[j, hc, :]) + pn[j, :, width + h * hd:width + (h + 1) * hd].astype(F32)
                zv = zv * lax.rsqrt(jnp.mean(zv * zv, -1, keepdims=True) + 1e-06)
                parts.append((zv * gall[j, h:h + 1, :]).astype(BF16))
        term = jnp.dot(jnp.concatenate(parts, 1), jnp.concatenate(blocks_w, 0), preferred_element_type=F32)
        if not first:
            term = total[:, :] + term
        if last:
            mixed[:, :] = term.astype(BF16)
        else:
            total[:, :] = term

    def gathered(*kinds):
        for kind in kinds:
            for c in range(nc):
                parrived(kind, c)

    gathered(2)
    state_landed(3)
    heads_of(0, True, False)
    for kind in range(3):
        state_landed(kind)
        state_copy(kind + 4).start()
    gathered(5, 6)
    state_landed(4)
    heads_of(Y - 1, False, False)
    state_landed(5)
    heads_of(1, False, False)
    gathered(7, 8)
    state_landed(6)
    heads_of(2, False, True)

    def drain(c, carry):
        sent(c)
        psent(c)
        return carry

    lax.fori_loop(0, nc, drain, 0)
    for kind in range(7):
        state_copy(kind).wait_send()
    for t in range(1, TP):
        y_copy(0, t).wait_send()
        y_copy(1, t).wait_send()
        gain_copy(t).wait_send()
    for t in range(1, X):
        ax_copy(t).wait_send()
        bx_copy(t).wait_send()
    for t in range(1, Z):
        bz_copy(t).wait_send()
    for k in range(8):
        az_copy(k).wait_send()
    for h in hs:
        @pl.when(z != root(h))
        def _():
            to_root(h).wait_send()

    @pl.when(is_root)
    def _():
        for d in range(1, X):
            @pl.when(x + d < X)
            def _():
                to_group(d).wait_send()
        for j in range(Z):
            @pl.when(z != j)
            def _():
                to_member(mine, j).wait_send()


def vmem_spec():
    return pl.BlockSpec(memory_space=pltpu.VMEM)


def local(hidden_in, w_qkv, lr_weight, inner_lr, init_state, norm_gain, w_out):
    rows, feat = hidden_in.shape
    _, depth, width = w_qkv.shape
    heads, hd = norm_gain.shape
    nc = rows // CH
    out_cols = w_out.shape[1] // TP
    dma = pltpu.SemaphoreType.DMA
    operands = (hidden_in, w_qkv, lr_weight.T, inner_lr, init_state, norm_gain, w_out)
    operands = [pltpu.with_memory_space_constraint(a, pltpu.HBM) for a in operands]
    return pl.pallas_call(
        layer_kernel,
        out_shape=jax.ShapeDtypeStruct((rows, out_cols), BF16),
        in_specs=[pl.BlockSpec(memory_space=pltpu.HBM)] * 7,
        out_specs=vmem_spec(),
        scratch_shapes=[
            pltpu.VMEM((heads, depth), BF16),
            pltpu.SMEM((heads,), F32),
            pltpu.VMEM((heads, hd, hd), F32),
            pltpu.VMEM((heads, hd), F32),
            pltpu.VMEM((TP, 8, hd), F32),
            pltpu.VMEM((TP, rows, feat), BF16),
            pltpu.VMEM((3, depth, width), BF16),
            pltpu.VMEM((depth, 8), BF16),
            pltpu.VMEM((8, depth), F32),
            pltpu.VMEM((rows, 3 * width + 8), F32),
            pltpu.VMEM((heads, hd, 2 * hd), F32),
            pltpu.VMEM((heads, hd, 2 * hd), BF16),
            pltpu.VMEM((Z, hd, 2 * hd), BF16),
            pltpu.VMEM((X, hd, 2 * hd), BF16),
            pltpu.VMEM((Z - 1, hd, 2 * hd), F32),
            pltpu.VMEM((hd, hd), F32),
            pltpu.VMEM((Z, hd, hd), BF16),
            pltpu.VMEM((TP, rows, 2 * width), BF16),
            pltpu.VMEM((TP, width, hd), BF16),
            pltpu.VMEM((Z, X, TP, MB, CH), BF16),
            pltpu.VMEM((X, Z, TP, MB, CH), BF16),
            pltpu.VMEM((rows, out_cols), F32),
            dma((3,)),
            dma((4,)),
            dma((3,)),
            dma((nc, 9)),
            dma((nc, 9)),
            dma((nc, 9)),
            dma((nc, 9)),
            dma((7,)),
            dma((7,)),
            dma((heads,)),
            dma((Z,)),
            dma((X - 1,)),
            dma((X,)),
            dma((Z,)),
            dma((heads,)),
            dma((3, TP - 1)),
            dma((3, TP - 1)),
            dma((X - 1,)),
            dma((X - 1,)),
            dma((8,)),
            dma((8,)),
            dma((Z - 1,)),
            dma((Z - 1,)),
            dma((X - 1,)),
            dma((X - 1,)),
        ],
        compiler_params=pltpu.CompilerParams(
            collective_id=0, has_side_effects=True, vmem_limit_bytes=48 * 1024 * 1024
        ),
        name="layer",
    )(*operands)


def solution(mesh):
    in_specs = (
        P("ctx", "tp"),
        P(None, None, "tp"),
        P(None, "tp"),
        P("tp"),
        P("tp", None, None),
        P("tp", None),
        P("tp", None),
    )
    out_specs = P("ctx", "tp")
    return jax.shard_map(local, mesh=mesh, in_specs=in_specs, out_specs=out_specs, check_vma=False)
```

```python
import jax
import jax.numpy as jnp
from jax import lax
from jax.experimental import pallas as pl
from jax.experimental.pallas import tpu as pltpu
from jax.sharding import PartitionSpec as P

MB = 16
CH = 128
MESH = pl.DeviceIdType.MESH
F32 = jnp.float32
BF16 = jnp.bfloat16
Y, CORES = 4, 2
X, Z = 4, 8
TP = Y * CORES


def dot(a, b):
    return jnp.dot(a.astype(BF16), b.astype(BF16), preferred_element_type=F32)


def compose(later, earlier, hd):
    return earlier + dot(later[:, :hd], earlier) + later


def apply_map(m, w, hd):
    return w + dot(m[:, :hd], w) + m[:, hd:]


def pair_gather(src, buf, span, me, send, recv):
    half = span // 2
    sib = me + 1 - 2 * lax.rem(me, 2)
    up, down, far = lax.rem(me + 2, TP), lax.rem(me + TP - 2, TP), lax.rem(me + 4, TP)
    sup, sdown, sfar = lax.rem(sib + 2, TP), lax.rem(sib + TP - 2, TP), lax.rem(sib + 4, TP)
    target = (up, down, sib, up, down, sib, sib, sib, sib)
    leaving = (me, me, me, down, up, down, up, far, far)
    landing = (down, up, sib, far, far, sdown, sup, sfar, sfar)

    def place(ref, kind, c, owner):
        r0 = half if kind in (4, 8) else 0
        n = half if kind in (3, 4, 7, 8) else span
        rs = pl.ds(pl.multiple_of(c * span + r0, 16), n)
        return ref.at[rs] if owner is None else ref.at[owner, rs]

    def out(kind, c):
        own = src is not None and kind < 3
        return pltpu.make_async_remote_copy(
            src_ref=place(src, kind, c, None) if own else place(buf, kind, c, leaving[kind]),
            dst_ref=place(buf, kind, c, leaving[kind]),
            send_sem=send.at[c, kind],
            recv_sem=recv.at[c, kind],
            device_id={"tp": target[kind]},
            device_id_type=MESH,
        )

    def arrived(kind, c):
        ref = place(buf, kind, c, landing[kind])
        pltpu.make_async_remote_copy(
            src_ref=ref, dst_ref=ref, send_sem=send.at[c, kind], recv_sem=recv.at[c, kind],
            device_id={"tp": sib}, device_id_type=MESH,
        ).wait_recv()

    def begin(c):
        out(0, c).start()
        out(1, c).start()

    def share(c):
        out(2, c).start()

    def forward(c):
        arrived(0, c)
        out(3, c).start()
        out(5, c).start()
        arrived(1, c)
        out(4, c).start()
        out(6, c).start()

    def far_forward(c):
        arrived(3, c)
        out(7, c).start()
        arrived(4, c)
        out(8, c).start()

    def sent(c):
        for kind in range(9):
            out(kind, c).wait_send()

    return begin, share, forward, far_forward, arrived, sent


def layer_kernel(hid, wq, lrw_in, lr_in, w0_in, gain_in, wout, mixed,
                 lrw, lr, w0, gain, gall, xg, wbuf, wgate, lrt, acc, pref, xbf, mbuf, tbuf, pre, prb, wst, wob, pn, wg, abuf, bbuf, total,
                 loc, lsem, wsem, gsend, grecv, psend, precv, hsend, hrecv, msend, mrecv, tsend, trecv, osend, orecv,
                 ysend, yrecv, axsend, axrecv, azsend, azrecv, bzsend, bzrecv, bxsend, bxrecv):
    rows, feat = hid.shape
    nc = rows // CH
    heads, hd = pref.shape[0], pref.shape[1]
    hs = range(heads)
    width = heads * hd
    ocols = mixed.shape[1]
    me = lax.axis_index("tp")
    ctx = lax.axis_index("ctx")
    core = lax.rem(me, 2)
    chip = me // 2
    z = lax.rem(ctx, Z)
    x = ctx // Z
    base = x * Z

    smalls = [
        pltpu.make_async_copy(a, b, lsem.at[i])
        for i, (a, b) in enumerate(((lrw_in, lrw), (lr_in, lr), (w0_in, w0), (gain_in, gain)))
    ]
    for cp in smalls:
        cp.start()
    barrier = pltpu.get_barrier_semaphore()
    for t in range(1, TP):
        pl.semaphore_signal(barrier, inc=1, device_id={"tp": lax.rem(me + t, TP)}, device_id_type=MESH)
    for t in range(1, Z):
        pl.semaphore_signal(barrier, inc=1, device_id={"ctx": base + lax.rem(z + t, Z)}, device_id_type=MESH)
    for t in range(1, X):
        pl.semaphore_signal(barrier, inc=1, device_id={"ctx": lax.rem(ctx + t * Z, X * Z)}, device_id_type=MESH)

    wcopies = [pltpu.make_async_copy(wq.at[c], wbuf.at[c], wsem.at[c]) for c in range(3)]
    for cp in wcopies:
        cp.start()
    own = pltpu.make_async_copy(hid, xg.at[me], loc.at[0])
    own.start()

    bblock = 8 + 2 * x + z // 4
    blocks = ((z, x), (bblock, lax.rem(z, 4)))

    def piece_in(kind, j):
        block, cb = blocks[kind]
        at = pl.multiple_of(j * ocols + cb * CH, CH)
        return wout.at[pl.ds(pl.multiple_of(block * MB, MB), MB), pl.ds(at, CH)]

    def piece(kind, j):
        return abuf.at[z, x, j] if kind == 0 else bbuf.at[x, z, j]

    def pieces(kind, cx, cz):
        return abuf.at[cz, cx] if kind == 0 else bbuf.at[cx, cz]

    def remote(src, dst, ss, rr, to):
        return pltpu.make_async_remote_copy(
            src_ref=src, dst_ref=dst, send_sem=ss, recv_sem=rr, device_id=to, device_id_type=MESH)

    def landed(ref, rr):
        remote(ref, ref, loc.at[0], rr, {"tp": lax.rem(me + 1, TP)}).wait_recv()

    def on_tp(t):
        return {"tp": lax.rem(me + t, TP)}

    def on_z(t):
        return {"ctx": base + lax.rem(z + t, Z)}

    def on_x(t):
        return {"ctx": lax.rem(ctx + t * Z, X * Z)}

    def y_copy(kind, t):
        return remote(piece_in(kind, lax.rem(me + t, TP)), piece(kind, me), ysend.at[kind, t - 1],
                      yrecv.at[kind, t - 1], on_tp(t))

    def gain_copy(t):
        return remote(gall.at[me], gall.at[me], ysend.at[2, t - 1], yrecv.at[2, t - 1], on_tp(t))

    def ax_copy(t):
        ref = pieces(0, x, z)
        return remote(ref, ref, axsend.at[t - 1], axrecv.at[t - 1], on_x(t))

    def bz_copy(t):
        ref = pieces(1, x, z)
        return remote(ref, ref, bzsend.at[t - 1], bzrecv.at[t - 1], on_z(t))

    def b_rows(cx):
        return bbuf.at[cx]

    def bx_copy(t):
        return remote(b_rows(x), b_rows(x), bxsend.at[t - 1], bxrecv.at[t - 1], on_x(t))

    az_hops = (1, 2, Z - 1, Z - 2, 1, Z - 1, 2, Z - 2)
    az_from = (0, 0, 0, 0, Z - 2, 2, Z - 2, 2)

    def az_ref(k, block):
        block = lax.rem(block + 2 * Z, Z)
        if k < 6:
            return abuf.at[block]
        return abuf.at[block, pl.ds((k - 6) * (X // 2), X // 2)]

    def az_copy(k):
        ref = az_ref(k, z + az_from[k])
        return remote(ref, ref, azsend.at[k], azrecv.at[k], on_z(az_hops[k]))

    def az_landed(k):
        landed(az_ref(k, z + az_from[k] - az_hops[k]), azrecv.at[k])

    def az_near():
        for k in (1, 3, 0, 2):
            az_copy(k).start()

    def az_far():
        az_landed(1)
        az_landed(3)
        for k in range(4, 8):
            az_copy(k).start()

    def spread_first():
        for t in range(1, TP):
            j = lax.rem(me + TP - t, TP)
            landed(piece(0, j), yrecv.at[0, t - 1])
            landed(piece(1, j), yrecv.at[1, t - 1])
        for cp in wown:
            cp.wait()
        for t in range(1, X):
            ax_copy(t).start()
        for t in range(1, Z):
            bz_copy(t).start()

    def spread_z():
        for t in range(1, X):
            landed(pieces(0, lax.rem(x + X - t, X), z), axrecv.at[t - 1])
        az_near()

    def spread_x():
        for t in range(1, Z):
            landed(pieces(1, x, lax.rem(z + Z - t, Z)), bzrecv.at[t - 1])
        for t in range(1, X):
            bx_copy(t).start()

    wown = [pltpu.make_async_copy(piece_in(kind, me), piece(kind, me), loc.at[1 + kind]) for kind in range(2)]
    for cp in wown:
        cp.start()
    begin, share, forward, far_forward, arrived, sent = pair_gather(hid, xg, CH, me, gsend, grecv)
    pbegin, pshare, pforward, pfar_forward, parrived, psent = pair_gather(None, pn, CH, me, psend, precv)
    pl.semaphore_wait(barrier, TP + Z + X - 3)
    begin(0)
    begin(1)
    for c in range(nc):
        share(c)

    lrt[...] = jnp.zeros_like(lrt)
    for cp in smalls:
        cp.wait()
    gall[me] = jnp.zeros_like(gall[me])
    gall[me, 0:heads, :] = gain[...]
    for t in range(1, TP):
        gain_copy(t).start()
    lrt[0:heads, :] = lrw[...].astype(F32)

    def gate(i, carry):
        at = pl.ds(pl.multiple_of(i * CH, CH), CH)
        wgate[at, :] = lrt[:, at].T.astype(BF16)
        return carry

    lax.fori_loop(0, wgate.shape[0] // CH, gate, 0)
    pref[...] = jnp.zeros_like(pref)
    for t in range(1, TP):
        y_copy(0, t).start()
        y_copy(1, t).start()
    own.wait()
    for cp in wcopies:
        cp.wait()

    def part(rs, q):
        cj = lax.rem(chip + q, Y)
        ks = pl.ds(pl.multiple_of(cj * 2 * feat, 2 * feat), 2 * feat)
        xs = jnp.concatenate([xg[2 * cj, rs], xg[2 * cj + 1, rs]], 1)
        weights = [wbuf[i, ks, :] for i in range(3)] + [wgate[ks, :]]
        return jnp.concatenate([jnp.dot(xs, w, preferred_element_type=F32) for w in weights], 1)

    def near():
        for c in range(nc):
            arrived(2, c)
        acc[...] = part(pl.ds(0, rows), 0)

    def sides(c):
        arrived(5, c)
        arrived(6, c)
        rs = pl.ds(pl.multiple_of(c * CH, CH), CH)
        acc[rs, :] += part(rs, 1) + part(rs, Y - 1)

    near()
    forward(0)
    begin(2)
    spread_first()
    sides(0)
    forward(1)
    begin(3)
    far_forward(0)
    sides(1)

    row = lax.broadcasted_iota(jnp.int32, (CH, CH), 0)
    col = lax.broadcasted_iota(jnp.int32, (CH, CH), 1)
    causal = row >= col
    before = (row >> 4) > (col >> 4)

    def chunk(c, carry):
        arrived(7, c)
        arrived(8, c)
        rs = pl.ds(pl.multiple_of(c * CH, CH), CH)
        proj = acc[rs, :] + part(rs, 2)
        part3 = [[proj[:, (k * heads + h) * hd:(k * heads + h + 1) * hd] for h in hs] for k in range(3)]

        def unit(v):
            return v * lax.rsqrt(jnp.sum(v * v, -1, keepdims=True) + hd * 1e-06)

        q = [unit(part3[0][h]) for h in hs]
        k = [unit(part3[1][h]) for h in hs]
        rate = [lr[h] * jax.nn.sigmoid(proj[:, 3 * width + h:3 * width + h + 1]) for h in hs]
        krt = [(k[h] * rate[h]).T.astype(BF16) for h in hs]
        qk = [jnp.concatenate([q[h], k[h]], 0).astype(BF16) for h in hs]
        sg = [dot(qk[h], krt[h]) for h in hs]
        x0 = [pref[h] for h in hs]
        qkx = [dot(qk[h], x0[h]) for h in hs]
        r = [qkx[h][CH:] + jnp.concatenate([k[h], -part3[2][h]], 1) for h in hs]
        m = [jnp.where(causal, sg[h][:CH], 0.0).astype(BF16) for h in hs]
        l1 = [jnp.where(before, sg[h][CH:], 0.0) for h in hs]
        lb = [l1[h].astype(BF16) for h in hs]
        l2 = [dot(lb[h], lb[h]) for h in hs]
        l34 = [dot(jnp.concatenate([lb[h], l2[h].astype(BF16)], 0), l2[h]) for h in hs]
        t1 = [l2[h] - l1[h] - l34[h][:CH] for h in hs]
        t = [t1[h] + l34[h][CH:] + dot(t1[h], l34[h][CH:]) for h in hs]
        e = [r[h] + dot(t[h], r[h]) for h in hs]
        dn = [dot(jnp.concatenate([krt[h], m[h]], 0), e[h]) for h in hs]
        for h in hs:
            pref[h] = x0[h] - dn[h][:CH]
            p = q[h] + qkx[h][:CH, :hd] - dn[h][CH:, :hd]
            n = qkx[h][:CH, hd:] - dn[h][CH:, hd:]
            pn[me, rs, h * hd:(h + 1) * hd] = p.astype(BF16)
            pn[me, rs, width + h * hd:width + (h + 1) * hd] = n.astype(BF16)

        @pl.when(c < nc - 2)
        def _():
            forward(c + 2)

        @pl.when(c < nc - 1)
        def _():
            far_forward(c + 1)

        @pl.when(c == nc - 2)
        def _():
            pbegin(2)
            pshare(2)

        @pl.when(c < nc - 2)
        def _():
            sides(c + 2)

        @pl.when(c == 1)
        def _():
            for k in range(2):
                pbegin(k)
                pshare(k)

        @pl.when(c == 0)
        def _():
            spread_z()

        @pl.when(c == 1)
        def _():
            spread_x()

        return carry

    lax.fori_loop(0, nc, chunk, 0)

    def root(h):
        return 4 * core + 2 * h

    def to_root(h):
        return pltpu.make_async_remote_copy(
            src_ref=xbf.at[h], dst_ref=mbuf.at[z], send_sem=msend.at[h], recv_sem=mrecv.at[z],
            device_id={"ctx": base + root(h)}, device_id_type=MESH,
        )

    for h in hs:
        xbf[h] = pref[h].astype(BF16)

        @pl.when(z != root(h))
        def _():
            to_root(h).start()

        @pl.when(z == root(h))
        def _():
            mbuf[z] = xbf[h]

    pbegin(nc - 1)
    pshare(nc - 1)
    pforward(0)
    pforward(1)

    def to_group(d):
        return remote(tbuf.at[x], tbuf.at[x], tsend.at[d - 1], trecv.at[x], on_x(d))

    def state_at(h):
        return wg.at[me, pl.ds(pl.multiple_of(h * hd, hd), hd)]

    def to_member(h, j):
        return remote(wob.at[j], state_at(h), osend.at[j], orecv.at[h], {"ctx": base + j})

    is_root = (z == root(0)) | (z == root(1))
    mine = lax.rem(z, 4) // 2

    @pl.when(is_root)
    def _():
        for j in range(Z):
            @pl.when(z != j)
            def _():
                landed(mbuf.at[j], mrecv.at[j])
        ms = [mbuf[j].astype(F32) for j in range(Z)]
        pr = [compose(ms[2 * j + 1], ms[2 * j], hd) for j in range(Z // 2)]
        qd = [compose(pr[2 * j + 1], pr[2 * j], hd) for j in range(Z // 4)]
        tbuf[x] = compose(qd[1], qd[0], hd).astype(BF16)
        for d in range(1, X):
            @pl.when(x + d < X)
            def _():
                to_group(d).start()
        six = compose(pr[2], qd[0], hd)
        for j, m in enumerate((ms[0], pr[0], compose(ms[2], pr[0], hd), qd[0], compose(ms[4], qd[0], hd), six,
                               compose(ms[6], six, hd))):
            pre[j] = m
            prb[j * hd:(j + 1) * hd, :] = m[:, :hd].astype(BF16)

    pforward(2)

    @pl.when(is_root)
    def _():
        wst[...] = w0[mine]
        for j in range(X - 1):
            @pl.when(j < x)
            def _():
                landed(tbuf.at[j], trecv.at[j])
                wst[...] = apply_map(tbuf[j].astype(F32), wst[...], hd)
        w = wst[...]
        prod = jnp.dot(prb[...], w.astype(BF16), preferred_element_type=F32)
        wob[0] = w.astype(BF16)
        for j in range(1, Z):
            wob[j] = (w + prod[(j - 1) * hd:j * hd] + pre[j - 1][:, hd:]).astype(BF16)
        for j in range(Z):
            @pl.when(z != j)
            def _():
                to_member(mine, j).start()
        wg[me, pl.ds(pl.multiple_of(mine * hd, hd), hd)] = wob[z]

    pforward(3)
    az_far()
    for c in range(nc):
        pfar_forward(c)
    far = {"tp": lax.rem(me + 4, TP)}
    sib = me + 1 - 2 * core
    hop = ({"tp": lax.rem(me + 2, TP)}, {"tp": lax.rem(me + TP - 2, TP)}, far) + ({"tp": sib},) * 4
    from_me = (0, 0, 0, 0, TP - 2, 2, 4)
    to_me = (me + TP - 2, me + 2, me + 4, sib, sib + TP - 2, sib + 2, sib + 4)

    def states(j, h):
        return wg.at[lax.rem(j, TP), pl.ds(h * hd, hd)]

    def state_copy(kind, h):
        ref = states(me + from_me[kind], h)
        return remote(ref, ref, hsend.at[kind, h], hrecv.at[kind, h], hop[kind])

    def state_landed(kind, h):
        landed(states(to_me[kind], h), hrecv.at[kind, h])

    for h in hs:
        @pl.when(z != root(h))
        def _():
            landed(state_at(h), orecv.at[h])
        for kind in (2, 0, 1, 3):
            state_copy(kind, h).start()
    for k in (0, 2, 4, 5, 6, 7):
        az_landed(k)
    for t in range(1, X):
        landed(b_rows(lax.rem(x + X - t, X)), bxrecv.at[t - 1])
    for t in range(1, TP):
        landed(gall.at[lax.rem(me + TP - t, TP)], yrecv.at[2, t - 1])

    def heads_of(q, first, last):
        cj = lax.rem(chip + q, Y)
        blocks_w, parts = [], []
        for k in range(2):
            j = 2 * cj + k
            top = [abuf[:, cx, j].reshape(CH, CH) for cx in range(X)]
            low = [jnp.concatenate([bbuf[cx, zr * 4 + cz, j] for cx in range(X) for zr in range(2)], 0)
                   for cz in range(4)]
            blocks_w += [jnp.concatenate(top, 1), jnp.concatenate(low, 1)]
            for h in hs:
                hc = slice(h * hd, (h + 1) * hd)
                zv = dot(pn[j, :, hc], wg[j, hc, :]) + pn[j, :, width + h * hd:width + (h + 1) * hd].astype(F32)
                zv = zv * lax.rsqrt(jnp.mean(zv * zv, -1, keepdims=True) + 1e-06)
                parts.append((zv * gall[j, h:h + 1, :]).astype(BF16))
        term = jnp.dot(jnp.concatenate(parts, 1), jnp.concatenate(blocks_w, 0), preferred_element_type=F32)
        if not first:
            term = total[:, :] + term
        if last:
            mixed[:, :] = term.astype(BF16)
        else:
            total[:, :] = term

    def gathered(*kinds):
        for kind in kinds:
            for c in range(nc):
                parrived(kind, c)

    gathered(2)
    for h in hs:
        state_landed(3, h)
    heads_of(0, True, False)
    for kind in range(3):
        for h in hs:
            state_landed(kind, h)
            state_copy(kind + 4, h).start()
    gathered(5, 6)
    for h in hs:
        state_landed(4, h)
    heads_of(Y - 1, False, False)
    for h in hs:
        state_landed(5, h)
    heads_of(1, False, False)
    gathered(7, 8)
    for h in hs:
        state_landed(6, h)
    heads_of(2, False, True)

    def drain(c, carry):
        sent(c)
        psent(c)
        return carry

    lax.fori_loop(0, nc, drain, 0)
    for kind in range(7):
        for h in hs:
            state_copy(kind, h).wait_send()
    for t in range(1, TP):
        y_copy(0, t).wait_send()
        y_copy(1, t).wait_send()
        gain_copy(t).wait_send()
    for t in range(1, X):
        ax_copy(t).wait_send()
        bx_copy(t).wait_send()
    for t in range(1, Z):
        bz_copy(t).wait_send()
    for k in range(8):
        az_copy(k).wait_send()
    for h in hs:
        @pl.when(z != root(h))
        def _():
            to_root(h).wait_send()

    @pl.when(is_root)
    def _():
        for d in range(1, X):
            @pl.when(x + d < X)
            def _():
                to_group(d).wait_send()
        for j in range(Z):
            @pl.when(z != j)
            def _():
                to_member(mine, j).wait_send()


def vmem_spec():
    return pl.BlockSpec(memory_space=pltpu.VMEM)


def local(hidden_in, w_qkv, lr_weight, inner_lr, init_state, norm_gain, w_out):
    rows, feat = hidden_in.shape
    _, depth, width = w_qkv.shape
    heads, hd = norm_gain.shape
    nc = rows // CH
    out_cols = w_out.shape[1] // TP
    dma = pltpu.SemaphoreType.DMA
    operands = (hidden_in, w_qkv, lr_weight.T, inner_lr, init_state, norm_gain, w_out)
    operands = [pltpu.with_memory_space_constraint(a, pltpu.HBM) for a in operands]
    return pl.pallas_call(
        layer_kernel,
        out_shape=jax.ShapeDtypeStruct((rows, out_cols), BF16),
        in_specs=[pl.BlockSpec(memory_space=pltpu.HBM)] * 7,
        out_specs=vmem_spec(),
        scratch_shapes=[
            pltpu.VMEM((heads, depth), BF16),
            pltpu.SMEM((heads,), F32),
            pltpu.VMEM((heads, hd, hd), F32),
            pltpu.VMEM((heads, hd), F32),
            pltpu.VMEM((TP, 8, hd), F32),
            pltpu.VMEM((TP, rows, feat), BF16),
            pltpu.VMEM((3, depth, width), BF16),
            pltpu.VMEM((depth, 8), BF16),
            pltpu.VMEM((8, depth), F32),
            pltpu.VMEM((rows, 3 * width + 8), F32),
            pltpu.VMEM((heads, hd, 2 * hd), F32),
            pltpu.VMEM((heads, hd, 2 * hd), BF16),
            pltpu.VMEM((Z, hd, 2 * hd), BF16),
            pltpu.VMEM((X, hd, 2 * hd), BF16),
            pltpu.VMEM((Z - 1, hd, 2 * hd), F32),
            pltpu.VMEM(((Z - 1) * hd, hd), BF16),
            pltpu.VMEM((hd, hd), F32),
            pltpu.VMEM((Z, hd, hd), BF16),
            pltpu.VMEM((TP, rows, 2 * width), BF16),
            pltpu.VMEM((TP, width, hd), BF16),
            pltpu.VMEM((Z, X, TP, MB, CH), BF16),
            pltpu.VMEM((X, Z, TP, MB, CH), BF16),
            pltpu.VMEM((rows, out_cols), F32),
            dma((3,)),
            dma((4,)),
            dma((3,)),
            dma((nc, 9)),
            dma((nc, 9)),
            dma((nc, 9)),
            dma((nc, 9)),
            dma((7, heads)),
            dma((7, heads)),
            dma((heads,)),
            dma((Z,)),
            dma((X - 1,)),
            dma((X,)),
            dma((Z,)),
            dma((heads,)),
            dma((3, TP - 1)),
            dma((3, TP - 1)),
            dma((X - 1,)),
            dma((X - 1,)),
            dma((8,)),
            dma((8,)),
            dma((Z - 1,)),
            dma((Z - 1,)),
            dma((X - 1,)),
            dma((X - 1,)),
        ],
        compiler_params=pltpu.CompilerParams(
            collective_id=0, has_side_effects=True, vmem_limit_bytes=48 * 1024 * 1024
        ),
        name="layer",
    )(*operands)


def solution(mesh):
    in_specs = (
        P("ctx", "tp"),
        P(None, None, "tp"),
        P(None, "tp"),
        P("tp"),
        P("tp", None, None),
        P("tp", None),
        P("tp", None),
    )
    out_specs = P("ctx", "tp")
    return jax.shard_map(local, mesh=mesh, in_specs=in_specs, out_specs=out_specs, check_vma=False)
```

```python
import jax
import jax.numpy as jnp
from jax import lax
from jax.experimental import pallas as pl
from jax.experimental.pallas import tpu as pltpu
from jax.sharding import PartitionSpec as P

MB = 16
CH = 128
MESH = pl.DeviceIdType.MESH
F32 = jnp.float32
BF16 = jnp.bfloat16
Y, CORES = 4, 2
X, Z = 4, 8
TP = Y * CORES


def dot(a, b):
    return jnp.dot(a.astype(BF16), b.astype(BF16), preferred_element_type=F32)


def compose(later, earlier, hd):
    return earlier + dot(later[:, :hd], earlier) + later


def apply_map(m, w, hd):
    return w + dot(m[:, :hd], w) + m[:, hd:]


def pair_gather(src, buf, span, me, send, recv):
    half = span // 2
    sib = me + 1 - 2 * lax.rem(me, 2)
    up, down, far = lax.rem(me + 2, TP), lax.rem(me + TP - 2, TP), lax.rem(me + 4, TP)
    sup, sdown, sfar = lax.rem(sib + 2, TP), lax.rem(sib + TP - 2, TP), lax.rem(sib + 4, TP)
    target = (up, down, sib, up, down, sib, sib, sib, sib)
    leaving = (me, me, me, down, up, down, up, far, far)
    landing = (down, up, sib, far, far, sdown, sup, sfar, sfar)

    def place(ref, kind, c, owner):
        r0 = half if kind in (4, 8) else 0
        n = half if kind in (3, 4, 7, 8) else span
        rs = pl.ds(pl.multiple_of(c * span + r0, 16), n)
        return ref.at[rs] if owner is None else ref.at[owner, rs]

    def out(kind, c):
        own = src is not None and kind < 3
        return pltpu.make_async_remote_copy(
            src_ref=place(src, kind, c, None) if own else place(buf, kind, c, leaving[kind]),
            dst_ref=place(buf, kind, c, leaving[kind]),
            send_sem=send.at[c, kind],
            recv_sem=recv.at[c, kind],
            device_id={"tp": target[kind]},
            device_id_type=MESH,
        )

    def arrived(kind, c):
        ref = place(buf, kind, c, landing[kind])
        pltpu.make_async_remote_copy(
            src_ref=ref, dst_ref=ref, send_sem=send.at[c, kind], recv_sem=recv.at[c, kind],
            device_id={"tp": sib}, device_id_type=MESH,
        ).wait_recv()

    def begin(c):
        out(0, c).start()
        out(1, c).start()

    def share(c):
        out(2, c).start()

    def forward(c):
        arrived(0, c)
        out(3, c).start()
        out(5, c).start()
        arrived(1, c)
        out(4, c).start()
        out(6, c).start()

    def far_forward(c):
        arrived(3, c)
        out(7, c).start()
        arrived(4, c)
        out(8, c).start()

    def sent(c):
        for kind in range(9):
            out(kind, c).wait_send()

    return begin, share, forward, far_forward, arrived, sent


def layer_kernel(hid, wq, lrw_in, lr_in, w0_in, gain_in, wout, mixed,
                 lrw, lr, w0, gain, gall, xg, wbuf, wgate, lrt, acc, pref, xbf, mbuf, tbuf, pre, prb, wst, wob, pn, wg, abuf, bbuf, total,
                 loc, lsem, wsem, gsend, grecv, psend, precv, hsend, hrecv, msend, mrecv, tsend, trecv, osend, orecv,
                 ysend, yrecv, axsend, axrecv, azsend, azrecv, bzsend, bzrecv, bxsend, bxrecv):
    rows, feat = hid.shape
    nc = rows // CH
    heads, hd = pref.shape[0], pref.shape[1]
    hs = range(heads)
    width = heads * hd
    ocols = mixed.shape[1]
    me = lax.axis_index("tp")
    ctx = lax.axis_index("ctx")
    core = lax.rem(me, 2)
    chip = me // 2
    z = lax.rem(ctx, Z)
    x = ctx // Z
    base = x * Z

    smalls = [
        pltpu.make_async_copy(a, b, lsem.at[i])
        for i, (a, b) in enumerate(((lrw_in, lrw), (lr_in, lr), (w0_in, w0), (gain_in, gain)))
    ]
    for cp in smalls:
        cp.start()
    barrier = pltpu.get_barrier_semaphore()
    for t in range(1, TP):
        pl.semaphore_signal(barrier, inc=1, device_id={"tp": lax.rem(me + t, TP)}, device_id_type=MESH)
    for t in range(1, Z):
        pl.semaphore_signal(barrier, inc=1, device_id={"ctx": base + lax.rem(z + t, Z)}, device_id_type=MESH)
    for t in range(1, X):
        pl.semaphore_signal(barrier, inc=1, device_id={"ctx": lax.rem(ctx + t * Z, X * Z)}, device_id_type=MESH)

    wcopies = [pltpu.make_async_copy(wq.at[c], wbuf.at[c], wsem.at[c]) for c in range(3)]
    for cp in wcopies:
        cp.start()
    own = pltpu.make_async_copy(hid, xg.at[me], loc.at[0])
    own.start()

    bblock = 8 + 2 * x + z // 4
    blocks = ((z, x), (bblock, lax.rem(z, 4)))

    def piece_in(kind, j):
        block, cb = blocks[kind]
        at = pl.multiple_of(j * ocols + cb * CH, CH)
        return wout.at[pl.ds(pl.multiple_of(block * MB, MB), MB), pl.ds(at, CH)]

    def piece(kind, j):
        return abuf.at[z, x, j] if kind == 0 else bbuf.at[x, z, j]

    def pieces(kind, cx, cz):
        return abuf.at[cz, cx] if kind == 0 else bbuf.at[cx, cz]

    def remote(src, dst, ss, rr, to):
        return pltpu.make_async_remote_copy(
            src_ref=src, dst_ref=dst, send_sem=ss, recv_sem=rr, device_id=to, device_id_type=MESH)

    def landed(ref, rr):
        remote(ref, ref, loc.at[0], rr, {"tp": lax.rem(me + 1, TP)}).wait_recv()

    def on_tp(t):
        return {"tp": lax.rem(me + t, TP)}

    def on_z(t):
        return {"ctx": base + lax.rem(z + t, Z)}

    def on_x(t):
        return {"ctx": lax.rem(ctx + t * Z, X * Z)}

    def y_copy(kind, t):
        return remote(piece_in(kind, lax.rem(me + t, TP)), piece(kind, me), ysend.at[kind, t - 1],
                      yrecv.at[kind, t - 1], on_tp(t))

    def gain_copy(t):
        return remote(gall.at[me], gall.at[me], ysend.at[2, t - 1], yrecv.at[2, t - 1], on_tp(t))

    def ax_copy(t):
        ref = pieces(0, x, z)
        return remote(ref, ref, axsend.at[t - 1], axrecv.at[t - 1], on_x(t))

    def bz_copy(t):
        ref = pieces(1, x, z)
        return remote(ref, ref, bzsend.at[t - 1], bzrecv.at[t - 1], on_z(t))

    def b_rows(cx):
        return bbuf.at[cx]

    def bx_copy(t):
        return remote(b_rows(x), b_rows(x), bxsend.at[t - 1], bxrecv.at[t - 1], on_x(t))

    az_hops = (1, 2, Z - 1, Z - 2, 1, Z - 1, 2, Z - 2)
    az_from = (0, 0, 0, 0, Z - 2, 2, Z - 2, 2)

    def az_ref(k, block):
        block = lax.rem(block + 2 * Z, Z)
        if k < 6:
            return abuf.at[block]
        return abuf.at[block, pl.ds((k - 6) * (X // 2), X // 2)]

    def az_copy(k):
        ref = az_ref(k, z + az_from[k])
        return remote(ref, ref, azsend.at[k], azrecv.at[k], on_z(az_hops[k]))

    def az_landed(k):
        landed(az_ref(k, z + az_from[k] - az_hops[k]), azrecv.at[k])

    def az_near():
        for k in (1, 3, 0, 2):
            az_copy(k).start()

    def az_far():
        az_landed(1)
        az_landed(3)
        for k in range(4, 8):
            az_copy(k).start()

    def spread_first():
        for t in range(1, TP):
            j = lax.rem(me + TP - t, TP)
            landed(piece(0, j), yrecv.at[0, t - 1])
            landed(piece(1, j), yrecv.at[1, t - 1])
        for cp in wown:
            cp.wait()
        for t in range(1, X):
            ax_copy(t).start()
        for t in range(1, Z):
            bz_copy(t).start()

    def spread_z():
        for t in range(1, X):
            landed(pieces(0, lax.rem(x + X - t, X), z), axrecv.at[t - 1])
        az_near()

    def spread_x():
        for t in range(1, Z):
            landed(pieces(1, x, lax.rem(z + Z - t, Z)), bzrecv.at[t - 1])
        for t in range(1, X):
            bx_copy(t).start()

    wown = [pltpu.make_async_copy(piece_in(kind, me), piece(kind, me), loc.at[1 + kind]) for kind in range(2)]
    for cp in wown:
        cp.start()
    begin, share, forward, far_forward, arrived, sent = pair_gather(hid, xg, CH, me, gsend, grecv)
    pbegin, pshare, pforward, pfar_forward, parrived, psent = pair_gather(None, pn, CH, me, psend, precv)
    pl.semaphore_wait(barrier, TP + Z + X - 3)
    begin(0)
    begin(1)
    for c in range(nc):
        share(c)

    lrt[...] = jnp.zeros_like(lrt)
    for cp in smalls:
        cp.wait()
    gall[me] = jnp.zeros_like(gall[me])
    gall[me, 0:heads, :] = gain[...]
    for t in range(1, TP):
        gain_copy(t).start()
    lrt[0:heads, :] = lrw[...].astype(F32)

    def gate(i, carry):
        at = pl.ds(pl.multiple_of(i * CH, CH), CH)
        wgate[at, :] = lrt[:, at].T.astype(BF16)
        return carry

    lax.fori_loop(0, wgate.shape[0] // CH, gate, 0)
    pref[...] = jnp.zeros_like(pref)
    for t in range(1, TP):
        y_copy(0, t).start()
        y_copy(1, t).start()
    own.wait()
    for cp in wcopies:
        cp.wait()

    def part(rs, q):
        cj = lax.rem(chip + q, Y)
        ks = pl.ds(pl.multiple_of(cj * 2 * feat, 2 * feat), 2 * feat)
        xs = jnp.concatenate([xg[2 * cj, rs], xg[2 * cj + 1, rs]], 1)
        weights = [wbuf[i, ks, :] for i in range(3)] + [wgate[ks, :]]
        return jnp.concatenate([jnp.dot(xs, w, preferred_element_type=F32) for w in weights], 1)

    def near():
        for c in range(nc):
            arrived(2, c)
        acc[...] = part(pl.ds(0, rows), 0)

    def sides(c):
        arrived(5, c)
        arrived(6, c)
        rs = pl.ds(pl.multiple_of(c * CH, CH), CH)
        acc[rs, :] += part(rs, 1) + part(rs, Y - 1)

    near()
    forward(0)
    begin(2)
    spread_first()
    sides(0)
    forward(1)
    begin(3)
    far_forward(0)
    sides(1)

    row = lax.broadcasted_iota(jnp.int32, (CH, CH), 0)
    col = lax.broadcasted_iota(jnp.int32, (CH, CH), 1)
    causal = row >= col
    before = (row >> 4) > (col >> 4)

    def chunk(c, carry):
        arrived(7, c)
        arrived(8, c)
        rs = pl.ds(pl.multiple_of(c * CH, CH), CH)
        proj = acc[rs, :] + part(rs, 2)
        part3 = [[proj[:, (k * heads + h) * hd:(k * heads + h + 1) * hd] for h in hs] for k in range(3)]

        def unit(v):
            return v * lax.rsqrt(jnp.sum(v * v, -1, keepdims=True) + hd * 1e-06)

        q = [unit(part3[0][h]) for h in hs]
        k = [unit(part3[1][h]) for h in hs]
        rate = [lr[h] * jax.nn.sigmoid(proj[:, 3 * width + h:3 * width + h + 1]) for h in hs]
        krt = [(k[h] * rate[h]).T.astype(BF16) for h in hs]
        qk = [jnp.concatenate([q[h], k[h]], 0).astype(BF16) for h in hs]
        sg = [dot(qk[h], krt[h]) for h in hs]
        x0 = [pref[h] for h in hs]
        qkx = [dot(qk[h], x0[h]) for h in hs]
        r = [qkx[h][CH:] + jnp.concatenate([k[h], -part3[2][h]], 1) for h in hs]
        m = [jnp.where(causal, sg[h][:CH], 0.0).astype(BF16) for h in hs]
        l1 = [jnp.where(before, sg[h][CH:], 0.0) for h in hs]
        lb = [l1[h].astype(BF16) for h in hs]
        l2 = [dot(lb[h], lb[h]) for h in hs]
        l34 = [dot(jnp.concatenate([lb[h], l2[h].astype(BF16)], 0), l2[h]) for h in hs]
        t1 = [l2[h] - l1[h] - l34[h][:CH] for h in hs]
        t = [t1[h] + l34[h][CH:] + dot(t1[h], l34[h][CH:]) for h in hs]
        e = [r[h] + dot(t[h], r[h]) for h in hs]
        dn = [dot(jnp.concatenate([krt[h], m[h]], 0), e[h]) for h in hs]
        for h in hs:
            pref[h] = x0[h] - dn[h][:CH]
            p = q[h] + qkx[h][:CH, :hd] - dn[h][CH:, :hd]
            n = qkx[h][:CH, hd:] - dn[h][CH:, hd:]
            pn[me, rs, h * hd:(h + 1) * hd] = p.astype(BF16)
            pn[me, rs, width + h * hd:width + (h + 1) * hd] = n.astype(BF16)

        @pl.when(c < nc - 2)
        def _():
            forward(c + 2)

        @pl.when(c < nc - 1)
        def _():
            far_forward(c + 1)

        @pl.when(c == nc - 2)
        def _():
            pbegin(2)
            pshare(2)

        @pl.when(c < nc - 2)
        def _():
            sides(c + 2)

        @pl.when(c == 1)
        def _():
            for k in range(2):
                pbegin(k)
                pshare(k)

        @pl.when(c == 0)
        def _():
            spread_z()

        @pl.when(c == 1)
        def _():
            spread_x()

        return carry

    lax.fori_loop(0, nc, chunk, 0)

    def root(h):
        return 4 * core + 2 * h

    def to_root(h):
        return pltpu.make_async_remote_copy(
            src_ref=xbf.at[h], dst_ref=mbuf.at[z], send_sem=msend.at[h], recv_sem=mrecv.at[z],
            device_id={"ctx": base + root(h)}, device_id_type=MESH,
        )

    for h in hs:
        xbf[h] = pref[h].astype(BF16)

        @pl.when(z != root(h))
        def _():
            to_root(h).start()

        @pl.when(z == root(h))
        def _():
            mbuf[z] = xbf[h]

    pbegin(nc - 1)
    pshare(nc - 1)
    pforward(0)
    pforward(1)

    def to_group(d):
        return remote(tbuf.at[x], tbuf.at[x], tsend.at[d - 1], trecv.at[x], on_x(d))

    def state_at(h):
        return wg.at[me, pl.ds(pl.multiple_of(h * hd, hd), hd)]

    def to_member(h, j):
        return remote(wob.at[j], state_at(h), osend.at[j], orecv.at[h], {"ctx": base + j})

    is_root = (z == root(0)) | (z == root(1))
    mine = lax.rem(z, 4) // 2

    @pl.when(is_root)
    def _():
        for j in range(Z):
            @pl.when(z != j)
            def _():
                landed(mbuf.at[j], mrecv.at[j])
        ms = [mbuf[j].astype(F32) for j in range(Z)]
        pr = [compose(ms[2 * j + 1], ms[2 * j], hd) for j in range(Z // 2)]
        qd = [compose(pr[2 * j + 1], pr[2 * j], hd) for j in range(Z // 4)]
        tbuf[x] = compose(qd[1], qd[0], hd).astype(BF16)
        @pl.when(x == 0)
        def _():
            tbuf[0, :, :hd] = apply_map(tbuf[0].astype(F32), w0[mine], hd).astype(BF16)

        for d in range(1, X):
            @pl.when(x + d < X)
            def _():
                to_group(d).start()
        six = compose(pr[2], qd[0], hd)
        for j, m in enumerate((ms[0], pr[0], compose(ms[2], pr[0], hd), qd[0], compose(ms[4], qd[0], hd), six,
                               compose(ms[6], six, hd))):
            pre[j] = m
            prb[j * hd:(j + 1) * hd, :] = m[:, :hd].astype(BF16)

    pforward(2)

    @pl.when(is_root)
    def _():
        wst[...] = w0[mine]
        for j in range(X - 1):
            @pl.when(j < x)
            def _():
                landed(tbuf.at[j], trecv.at[j])
                m = tbuf[j].astype(F32)
                wst[...] = m[:, :hd] if j == 0 else apply_map(m, wst[...], hd)
        w = wst[...]
        prod = jnp.dot(prb[...], w.astype(BF16), preferred_element_type=F32)
        wob[0] = w.astype(BF16)
        for j in range(1, Z):
            wob[j] = (w + prod[(j - 1) * hd:j * hd] + pre[j - 1][:, hd:]).astype(BF16)
        for j in range(Z):
            @pl.when(z != j)
            def _():
                to_member(mine, j).start()
        wg[me, pl.ds(pl.multiple_of(mine * hd, hd), hd)] = wob[z]

    pforward(3)
    az_far()
    for c in range(nc):
        pfar_forward(c)
    far = {"tp": lax.rem(me + 4, TP)}
    sib = me + 1 - 2 * core
    hop = ({"tp": lax.rem(me + 2, TP)}, {"tp": lax.rem(me + TP - 2, TP)}, far) + ({"tp": sib},) * 4
    from_me = (0, 0, 0, 0, TP - 2, 2, 4)
    to_me = (me + TP - 2, me + 2, me + 4, sib, sib + TP - 2, sib + 2, sib + 4)

    def states(j, h):
        return wg.at[lax.rem(j, TP), pl.ds(h * hd, hd)]

    def state_copy(kind, h):
        ref = states(me + from_me[kind], h)
        return remote(ref, ref, hsend.at[kind, h], hrecv.at[kind, h], hop[kind])

    def state_landed(kind, h):
        landed(states(to_me[kind], h), hrecv.at[kind, h])

    for h in hs:
        @pl.when(z != root(h))
        def _():
            landed(state_at(h), orecv.at[h])
        for kind in (2, 0, 1, 3):
            state_copy(kind, h).start()
    for k in (0, 2, 4, 5, 6, 7):
        az_landed(k)
    for t in range(1, X):
        landed(b_rows(lax.rem(x + X - t, X)), bxrecv.at[t - 1])
    for t in range(1, TP):
        landed(gall.at[lax.rem(me + TP - t, TP)], yrecv.at[2, t - 1])

    def heads_of(q, first, last):
        cj = lax.rem(chip + q, Y)
        blocks_w, parts = [], []
        for k in range(2):
            j = 2 * cj + k
            top = [abuf[:, cx, j].reshape(CH, CH) for cx in range(X)]
            low = [jnp.concatenate([bbuf[cx, zr * 4 + cz, j] for cx in range(X) for zr in range(2)], 0)
                   for cz in range(4)]
            blocks_w += [jnp.concatenate(top, 1), jnp.concatenate(low, 1)]
            for h in hs:
                hc = slice(h * hd, (h + 1) * hd)
                zv = dot(pn[j, :, hc], wg[j, hc, :]) + pn[j, :, width + h * hd:width + (h + 1) * hd].astype(F32)
                zv = zv * lax.rsqrt(jnp.mean(zv * zv, -1, keepdims=True) + 1e-06)
                parts.append((zv * gall[j, h:h + 1, :]).astype(BF16))
        term = jnp.dot(jnp.concatenate(parts, 1), jnp.concatenate(blocks_w, 0), preferred_element_type=F32)
        if not first:
            term = total[:, :] + term
        if last:
            mixed[:, :] = term.astype(BF16)
        else:
            total[:, :] = term

    def gathered(*kinds):
        for kind in kinds:
            for c in range(nc):
                parrived(kind, c)

    gathered(2)
    for h in hs:
        state_landed(3, h)
    heads_of(0, True, False)
    for kind in range(3):
        for h in hs:
            state_landed(kind, h)
            state_copy(kind + 4, h).start()
    gathered(5, 6)
    for h in hs:
        state_landed(4, h)
    heads_of(Y - 1, False, False)
    for h in hs:
        state_landed(5, h)
    heads_of(1, False, False)
    gathered(7, 8)
    for h in hs:
        state_landed(6, h)
    heads_of(2, False, True)

    def drain(c, carry):
        sent(c)
        psent(c)
        return carry

    lax.fori_loop(0, nc, drain, 0)
    for kind in range(7):
        for h in hs:
            state_copy(kind, h).wait_send()
    for t in range(1, TP):
        y_copy(0, t).wait_send()
        y_copy(1, t).wait_send()
        gain_copy(t).wait_send()
    for t in range(1, X):
        ax_copy(t).wait_send()
        bx_copy(t).wait_send()
    for t in range(1, Z):
        bz_copy(t).wait_send()
    for k in range(8):
        az_copy(k).wait_send()
    for h in hs:
        @pl.when(z != root(h))
        def _():
            to_root(h).wait_send()

    @pl.when(is_root)
    def _():
        for d in range(1, X):
            @pl.when(x + d < X)
            def _():
                to_group(d).wait_send()
        for j in range(Z):
            @pl.when(z != j)
            def _():
                to_member(mine, j).wait_send()


def vmem_spec():
    return pl.BlockSpec(memory_space=pltpu.VMEM)


def local(hidden_in, w_qkv, lr_weight, inner_lr, init_state, norm_gain, w_out):
    rows, feat = hidden_in.shape
    _, depth, width = w_qkv.shape
    heads, hd = norm_gain.shape
    nc = rows // CH
    out_cols = w_out.shape[1] // TP
    dma = pltpu.SemaphoreType.DMA
    operands = (hidden_in, w_qkv, lr_weight.T, inner_lr, init_state, norm_gain, w_out)
    operands = [pltpu.with_memory_space_constraint(a, pltpu.HBM) for a in operands]
    return pl.pallas_call(
        layer_kernel,
        out_shape=jax.ShapeDtypeStruct((rows, out_cols), BF16),
        in_specs=[pl.BlockSpec(memory_space=pltpu.HBM)] * 7,
        out_specs=vmem_spec(),
        scratch_shapes=[
            pltpu.VMEM((heads, depth), BF16),
            pltpu.SMEM((heads,), F32),
            pltpu.VMEM((heads, hd, hd), F32),
            pltpu.VMEM((heads, hd), F32),
            pltpu.VMEM((TP, 8, hd), F32),
            pltpu.VMEM((TP, rows, feat), BF16),
            pltpu.VMEM((3, depth, width), BF16),
            pltpu.VMEM((depth, 8), BF16),
            pltpu.VMEM((8, depth), F32),
            pltpu.VMEM((rows, 3 * width + 8), F32),
            pltpu.VMEM((heads, hd, 2 * hd), F32),
            pltpu.VMEM((heads, hd, 2 * hd), BF16),
            pltpu.VMEM((Z, hd, 2 * hd), BF16),
            pltpu.VMEM((X, hd, 2 * hd), BF16),
            pltpu.VMEM((Z - 1, hd, 2 * hd), F32),
            pltpu.VMEM(((Z - 1) * hd, hd), BF16),
            pltpu.VMEM((hd, hd), F32),
            pltpu.VMEM((Z, hd, hd), BF16),
            pltpu.VMEM((TP, rows, 2 * width), BF16),
            pltpu.VMEM((TP, width, hd), BF16),
            pltpu.VMEM((Z, X, TP, MB, CH), BF16),
            pltpu.VMEM((X, Z, TP, MB, CH), BF16),
            pltpu.VMEM((rows, out_cols), F32),
            dma((3,)),
            dma((4,)),
            dma((3,)),
            dma((nc, 9)),
            dma((nc, 9)),
            dma((nc, 9)),
            dma((nc, 9)),
            dma((7, heads)),
            dma((7, heads)),
            dma((heads,)),
            dma((Z,)),
            dma((X - 1,)),
            dma((X,)),
            dma((Z,)),
            dma((heads,)),
            dma((3, TP - 1)),
            dma((3, TP - 1)),
            dma((X - 1,)),
            dma((X - 1,)),
            dma((8,)),
            dma((8,)),
            dma((Z - 1,)),
            dma((Z - 1,)),
            dma((X - 1,)),
            dma((X - 1,)),
        ],
        compiler_params=pltpu.CompilerParams(
            collective_id=0, has_side_effects=True, vmem_limit_bytes=48 * 1024 * 1024
        ),
        name="layer",
    )(*operands)


def solution(mesh):
    in_specs = (
        P("ctx", "tp"),
        P(None, None, "tp"),
        P(None, "tp"),
        P("tp"),
        P("tp", None, None),
        P("tp", None),
        P("tp", None),
    )
    out_specs = P("ctx", "tp")
    return jax.shard_map(local, mesh=mesh, in_specs=in_specs, out_specs=out_specs, check_vma=False)
```
